32 devices in a mesh: occ: 4 (over y, x), vir: 8 (over z, core).
Axes of the slice: x: 2, y: 2, z: 4, core: 2. Of those that a mesh axis runs over, the one named last changes fastest.
Arguments:
- amplitudes: bfloat16 [32, 32, 589824], P(None, None, ('occ', 'vir')), may hold values from -6 to 6
- ladder_integrals: bfloat16 [32, 32, 589824], P(None, None, ('occ', 'vir')), may hold values from -0.015625 to 0.015625
- driver: float32 [32, 32, 1024], P('occ', 'vir'), may hold values from -6 to 6
- occ_energy: float32 [32], replicated, may hold values from -2 to -0.5
- vir_energy: float32 [32], replicated, may hold values from 0.5 to 4
- occ_irrep: int32 [32], replicated, may hold values from 0 to 3
- vir_tile_irrep: int32 [12], replicated, may hold values from 0 to 3
Outputs:
- updated: float32 [32, 32, 1024], P('occ', 'vir')
The draws below stay inside these ranges and needn't reach their ends.
All inputs are finite; a program needn't handle non-finite values.
Results may differ from the reference program's by a relative error of at most 0.0003.
Values sent between devices are 32-bit elements; how exact they have to be, the bound alone decides.
No kernel may reach another device: no remote copies, remote signals or barrier semaphores. Data moves between devices by JAX's collectives and lax.ppermute only.
A program may use at most 192 MiB of HBM per device.

```python
import jax
import jax.numpy as jnp
from jax import lax

NV = 768
TILE = 64
NO_W = 32
NA = 32
N_OCC = 4
N_VIR = 8


def touch_ends(values, stream_key, low, high):
    longest = values.shape.index(max(values.shape))
    spots = []
    for shift in (0, 1):
        where = [jax.random.randint(jax.random.fold_in(stream_key, axis), (), 0, length) for axis, length in enumerate(values.shape)]
        where[longest] = (where[longest] + shift) % values.shape[longest]
        spots.append(tuple(where))
    return values.at[spots[0]].set(low).at[spots[1]].set(high)


def raised(values, own_key, source, target, blocks, factor):
    owner, partner = [(jnp.arange(values.shape[dim]) // (values.shape[dim] // blocks)).reshape([-1 if axis == dim else 1 for axis in range(values.ndim)]) for dim in (source, target)]
    chosen = jax.random.permutation(own_key, blocks)[partner]
    strong = (owner == chosen) | (owner == (partner + blocks // 2) % blocks)
    return jnp.where(strong, factor * values, values)


def shard_levels(stream_key, dims, pieces, smallest, top_value):
    def one(dim, shards_of):
        steps = jax.random.uniform(jax.random.fold_in(jax.random.fold_in(stream_key, 6), dim), (shards_of,), jnp.float32, smallest / len(pieces), top_value / len(pieces))
        return jnp.repeat(jnp.exp(steps), dims[dim] // shards_of).reshape((-1,) + (1,) * (len(dims) - dim - 1))

    factor_of = one(*pieces[0])
    for cut in pieces[1:]:
        factor_of = factor_of * one(*cut)
    return factor_of


def scatter_about(own_key, extent, deviation, most, cuts=(), held_as=jnp.bfloat16):
    entries = jax.random.normal(own_key, extent, jnp.float32) * deviation
    if len(cuts) > 0:
        entries = shard_levels(own_key, extent, cuts, -0.22, 0.18) * entries
    return jnp.clip(entries, min=-most, max=most).astype(held_as)


def noise_with(stream_key, extent, width, reach, split, heavy, kind=jnp.bfloat16):
    drawn = width * jax.random.normal(stream_key, extent, jnp.float32)
    if split:
        drawn = drawn * shard_levels(stream_key, extent, split, -0.22, 0.18)
    return jnp.clip(raised(drawn, jax.random.fold_in(stream_key, 3), *heavy), -reach, reach).astype(kind)


def setup_inputs(seed: int = 0) -> dict:
    arg_keys = jax.random.split(jax.random.key(seed), 8)
    amplitudes = scatter_about(arg_keys[0], (NO_W, NO_W, NV * NV), 1.0, 6.0, ((2, 32),))
    ladder_integrals = noise_with(arg_keys[1], (NA, NA, NV * NV), (NV * NV) ** -0.5, 0.015625, ((2, 32),), (2, 0, 32, 2.75))
    driver = scatter_about(arg_keys[2], (NO_W, NA, NO_W * NA), 1.0, 6.0, ((0, 4), (1, 8)), jnp.float32)
    occ_energy = jnp.clip(jax.random.uniform(arg_keys[3], (NO_W,), jnp.float32, -2.0, -0.5), -2.0, -0.5)
    vir_energy = jnp.clip(jax.random.uniform(arg_keys[4], (NA,), jnp.float32, 0.5, 4.0), 0.5, 4.0)
    occ_irrep = touch_ends(jax.random.randint(arg_keys[5], (NO_W,), 0, 4), jax.random.fold_in(arg_keys[5], 1), 0, 3).astype(jnp.int32)
    vir_tile_irrep = touch_ends(jax.random.randint(arg_keys[6], (NV // TILE,), 0, 4), jax.random.fold_in(arg_keys[6], 1), 0, 3).astype(jnp.int32)
    return {"amplitudes": amplitudes, "ladder_integrals": ladder_integrals, "driver": driver, "occ_energy": occ_energy, "vir_energy": vir_energy, "occ_irrep": occ_irrep, "vir_tile_irrep": vir_tile_irrep}


def cd_labels(positions, labels):
    tiles = jnp.arange(labels.shape[0], dtype=jnp.int32)
    first = (positions // NV) // TILE
    second = (positions % NV) // TILE
    lab_first = jnp.sum(jnp.where(first[:, None] == tiles[None, :], labels[None, :], 0), axis=1)
    lab_second = jnp.sum(jnp.where(second[:, None] == tiles[None, :], labels[None, :], 0), axis=1)
    return jnp.bitwise_xor(lab_first, lab_second).astype(jnp.int32)


def reference(amplitudes, ladder_integrals, driver, occ_energy, vir_energy, occ_irrep, vir_tile_irrep):
    total_cd = NV * NV
    blocks = N_OCC * N_VIR
    block_width = total_cd // blocks
    pair_label = jnp.bitwise_xor(occ_irrep[:, None], occ_irrep[None, :]).reshape(-1)
    amp_rows = amplitudes.reshape(NO_W * NO_W, total_cd)
    int_rows = ladder_integrals.reshape(NA * NA, total_cd)

    def step(block, acc):
        start = (block * block_width).astype(jnp.int32)
        positions = start + jnp.arange(block_width, dtype=jnp.int32)
        labels = cd_labels(positions, vir_tile_irrep)
        keep = jnp.bitwise_xor(pair_label[:, None], labels[None, :]) == 0
        amp_block = lax.dynamic_slice_in_dim(amp_rows, start, block_width, 1)
        masked = jnp.where(keep, amp_block, jnp.zeros_like(amp_block))
        int_block = lax.dynamic_slice_in_dim(int_rows, start, block_width, 1)
        return acc + jnp.dot(masked, int_block.T, preferred_element_type=jnp.float32)

    acc = lax.fori_loop(0, blocks, step, jnp.zeros((NO_W * NO_W, NA * NA), jnp.float32))
    ladder = acc.reshape(NO_W, NO_W, NA, NA)
    paired = ladder + ladder.transpose(1, 0, 3, 2)
    ordered = paired.transpose(0, 2, 1, 3)
    denom = (occ_energy[:, None, None, None] + occ_energy[None, None, :, None]
             - vir_energy[None, :, None, None] - vir_energy[None, None, None, :])
    result = (driver.reshape(NO_W, NA, NO_W, NA) + ordered) / denom
    return result.reshape(NO_W, NA, NO_W * NA)
```

```python
import functools
import math

import jax
import jax.numpy as jnp
from jax import lax
from jax.experimental import pallas as pl
from jax.experimental.pallas import tpu as pltpu
from jax.sharding import PartitionSpec as P

NV = 768
TILE = 64
LANES = 128
IRREPS = 4
SIZES = (10, 12)
CHUNK = 16


def ladder_kernel(occ_irrep, vir_irrep, place, ycode_ref, *refs, cs, width, occ_local, steps):
    t_refs, v_refs = refs[:cs], refs[cs:2 * cs]
    keep_ref, send_ref = refs[2 * cs:2 * cs + 2]
    acc, tp, zs, xs, codes, table, slot_of, count = refs[2 * cs + 2:]
    occupied, _, _ = t_refs[0].shape
    virtual = v_refs[0].shape[0]
    tiles = virtual * virtual // LANES
    per_tile = LANES // virtual
    k, g = pl.program_id(0), pl.program_id(1)
    groups = pl.num_programs(1)
    first_half = lax.broadcasted_iota(jnp.int32, (occupied, LANES), 1) < LANES // 2

    @pl.when((k == 0) & (g == 0))
    def _():
        for x in range(IRREPS):
            count[x] = 0

        @pl.loop(0, table.shape[0])
        def _(s):
            table[s] = 0

        @pl.loop(0, occupied)
        def _(i):
            x = occ_irrep[i]
            s = count[x]
            table[s * IRREPS + x] = i
            slot_of[i] = s
            count[x] = s + 1

        most = jnp.maximum(jnp.maximum(count[0], count[1]), jnp.maximum(count[2], count[3]))
        count[IRREPS] = most
        for label in range(IRREPS):
            codes[label] = jnp.bitwise_xor(ycode_ref[...], label).astype(jnp.float32).astype(jnp.bfloat16)

        @pl.loop(0, most)
        def _(s):
            rows = pl.ds(pl.multiple_of(s * occupied, occupied), occupied)
            for label in range(IRREPS):
                for tile in range(tiles):
                    acc[label, tile, rows, :] = jnp.zeros((occupied, LANES), jnp.float32)

    most = count[IRREPS]
    c_tile = (place[0] + k * cs) // TILE
    c_label = vir_irrep[c_tile]

    def paired(first, second, mask):
        turned = pltpu.roll(second, LANES // 2, 1)
        return jnp.where(mask, first, turned), jnp.where(mask, turned, first)

    def work(size, base):
        rows_all = size * occupied

        @pl.loop(0, width // LANES)
        def _(m):
            lanes = pl.ds(pl.multiple_of(m * LANES, LANES), LANES)
            d_tile = 2 * (g * (width // LANES) + m)
            labels = [jnp.bitwise_xor(c_label, vir_irrep[d_tile + h]) for h in range(2)]
            z = jnp.where(first_half, codes[labels[0]], codes[labels[1]])
            masks = [z == x for x in range(IRREPS - 1)]
            for s in range(size):
                ids = [table[(base + s) * IRREPS + x] for x in range(IRREPS)]
                merged = []
                for c in range(cs):
                    out = t_refs[c][ids[IRREPS - 1], :, lanes]
                    for x in range(IRREPS - 1):
                        out = jnp.where(masks[x], t_refs[c][ids[x], :, lanes], out)
                    merged.append(out)
                for p in range(cs // 2):
                    halves = paired(merged[2 * p], merged[2 * p + 1], first_half)
                    for h in range(2):
                        tp[h, s * occupied:(s + 1) * occupied, p * LANES:(p + 1) * LANES] = halves[h]
            band = 2 * LANES // virtual
            wide = lax.broadcasted_iota(jnp.int32, (2 * LANES, LANES), 1) < LANES // 2
            for n in range(virtual // band):
                blocks = [v_refs[c][n * band:(n + 1) * band, :, lanes].reshape(2 * LANES, LANES) for c in range(cs)]
                pairs = [paired(blocks[2 * p], blocks[2 * p + 1], wide) for p in range(cs // 2)]
                for h in range(2):
                    weights = jnp.concatenate([pair[h] for pair in pairs], axis=1)
                    part = lax.dot_general(
                        tp[h, :rows_all, :], weights, (((1,), (1,)), ((), ())),
                        preferred_element_type=jnp.float32,
                    )
                    at = pl.ds(pl.multiple_of(base * occupied, occupied), rows_all)
                    acc[labels[h], 2 * n, at, :] += part[:, :LANES]
                    acc[labels[h], 2 * n + 1, at, :] += part[:, LANES:]

    low = 0
    for size in SIZES:
        @pl.when((most > low) & (most <= size))
        def _(size=size):
            work(size, 0)
        low = size

    @pl.when(most > low)
    def _():
        @pl.loop(0, (most + CHUNK - 1) // CHUNK)
        def _(r):
            work(CHUNK, r * CHUNK)

    @pl.when((k == steps - 1) & (g == groups - 1))
    def _():
        @pl.loop(0, occupied)
        def _(i):
            x = occ_irrep[i]
            rows = pl.ds(pl.multiple_of(slot_of[i] * occupied, occupied), occupied)
            to = pl.ds(pl.multiple_of(i * occupied, occupied), occupied)
            hit = [ycode_ref[...] == jnp.bitwise_xor(x, label) for label in range(IRREPS - 1)]
            for tile in range(tiles):
                out = acc[IRREPS - 1, tile, rows, :]
                for label in range(IRREPS - 1):
                    out = jnp.where(hit[label], acc[label, tile, rows, :], out)
                xs[tile, to, :] = out

        @pl.loop(0, occupied * occupied // LANES)
        def _(r):
            rows = pl.ds(pl.multiple_of(r * LANES, LANES), LANES)
            for tile in range(tiles):
                zs[tile * LANES:(tile + 1) * LANES, :] = xs[tile, rows, :].T
            for tile in range(tiles):
                mixed = jnp.concatenate(
                    [zs[pl.ds(tile * per_tile + b, virtual, stride=virtual), :] for b in range(per_tile)], axis=0
                )
                acc[0, tile, rows, :] = mixed.T

        @pl.loop(0, occupied)
        def _(i):
            there = jnp.bitwise_xor(i // occ_local, place[1])
            to = pl.ds(pl.multiple_of((there * occ_local + i % occ_local) * occupied, occupied), occupied)
            rows = pl.ds(pl.multiple_of(i * occupied, occupied), occupied)
            for tile in range(tiles):
                value = xs[tile, rows, :] + acc[0, tile, pl.ds(i, occupied, stride=occupied), :]
                far = jnp.bitwise_xor(tile, place[2])

                @pl.when(far % 2 == 0)
                def _():
                    keep_ref[far // 2, to, :] = value

                @pl.when(far % 2 == 1)
                def _():
                    send_ref[far // 2, to, :] = value


def ladder(amplitudes, ladder_integrals, occ_irrep, vir_tile_irrep, first_c, occ_at, vir_at, occ_local):
    occupied, _, cd_local = amplitudes.shape
    virtual = ladder_integrals.shape[0]
    local_c = cd_local // NV
    cs = math.gcd(local_c, TILE, 4)
    assert cs % 2 == 0 and local_c * NV == cd_local and occupied == virtual and LANES % virtual == 0
    width = NV // 2
    groups = NV // width
    steps = local_c // cs
    tiles = virtual * virtual // LANES
    place = jnp.stack([first_c, occ_at, vir_at]).astype(jnp.int32)
    ycode = jnp.broadcast_to(occ_irrep[:, None], (occupied, LANES)).astype(jnp.int32)

    def columns(c):
        return pl.BlockSpec((occupied, occupied, width), lambda k, g, *_: (0, 0, (k * cs + c) * groups + g))

    half = jax.ShapeDtypeStruct((tiles // 2, occupied * occupied, LANES), jnp.float32)
    half_spec = pl.BlockSpec(half.shape, lambda k, g, *_: (0, 0, 0))
    slots = -(-occupied // CHUNK) * CHUNK
    return pl.pallas_call(
        functools.partial(ladder_kernel, cs=cs, width=width, occ_local=occ_local, steps=steps),
        out_shape=(half, half),
        grid_spec=pltpu.PrefetchScalarGridSpec(
            num_scalar_prefetch=3,
            grid=(steps, groups),
            in_specs=[pl.BlockSpec((occupied, LANES), lambda k, g, *_: (0, 0))]
            + [columns(c) for c in range(cs)] * 2,
            out_specs=(half_spec, half_spec),
            scratch_shapes=[
                pltpu.VMEM((IRREPS, tiles, slots * occupied, LANES), jnp.float32),
                pltpu.VMEM((2, CHUNK * occupied, cs // 2 * LANES), jnp.bfloat16),
                pltpu.VMEM((tiles * LANES, LANES), jnp.float32),
                pltpu.VMEM((tiles, occupied * occupied, LANES), jnp.float32),
                pltpu.VMEM((IRREPS, occupied, LANES), jnp.bfloat16),
                pltpu.SMEM((slots * IRREPS,), jnp.int32),
                pltpu.SMEM((occupied,), jnp.int32),
                pltpu.SMEM((8,), jnp.int32),
            ],
        ),
        compiler_params=pltpu.CompilerParams(
            dimension_semantics=("arbitrary", "arbitrary"), vmem_limit_bytes=56 * 1024 * 1024
        ),
    )(occ_irrep, vir_tile_irrep, place, ycode, *([amplitudes] * cs), *([ladder_integrals] * cs))


def swap(values, axis, bit):
    size = lax.axis_size(axis)
    return lax.ppermute(values, axis, [(n, n ^ bit) for n in range(size)])


def halved(kept, got, axis, bits):
    for bit in bits:
        far = sum(part[1] for part in kept)
        near = [part[0] for part in kept]
        kept = near + [swap(far, axis, bit)]
    return sum(kept)


def owned_sum(keep, send, occ_groups, vir_groups, occ_local, occupied):
    zs = vir_groups // 2
    rows = occ_local // 2 * occupied

    def cut(values, part):
        split = values.reshape(zs, occ_groups, 2, rows, LANES)
        return split[:, :, part]

    done = []
    for part in range(2):
        kept = [cut(keep, part), swap(cut(send, part), "vir", 1)]
        kept = [v.transpose(1, 0, 2, 3).reshape(2, 2, zs, rows, LANES) for v in kept]
        if part:
            kept = [v.transpose(1, 0, 2, 3, 4) for v in kept]
            value = halved(kept, None, "occ", (1, 2))
        else:
            value = halved(kept, None, "occ", (2, 1))
        value = value.reshape(2, 2, rows, LANES).transpose(1, 0, 2, 3)
        done.append(halved([value], None, "vir", (2, 4)))
    return jnp.stack(done)


def local(amplitudes, ladder_integrals, driver, occ_energy, vir_energy, occ_irrep, vir_tile_irrep):
    occ_groups = lax.axis_size("occ")
    vir_groups = lax.axis_size("vir")
    occupied = amplitudes.shape[0]
    virtual = ladder_integrals.shape[0]
    occ_local = occupied // occ_groups
    vir_local = virtual // vir_groups
    rank = lax.axis_index(("occ", "vir"))
    occ_rank = lax.axis_index("occ")
    vir_rank = lax.axis_index("vir")
    first_c = rank * (amplitudes.shape[2] // NV)
    tiles = virtual * virtual // LANES
    direct = vir_groups == tiles == 8 and occ_groups == 4
    here = (occ_rank, vir_rank) if direct else (0 * occ_rank, 0 * vir_rank)
    keep, send = ladder(amplitudes, ladder_integrals, occ_irrep, vir_tile_irrep, first_c, *here, occ_local)
    if direct:
        owned = owned_sum(keep, send, occ_groups, vir_groups, occ_local, occupied)
        owned = owned.reshape(occ_local, occupied, vir_local, virtual)
    else:
        term = jnp.stack([keep, send], axis=1).reshape(
            tiles, occ_groups, occ_local, occupied, vir_groups // tiles, vir_local, virtual
        )
        term = term.transpose(1, 0, 4, 2, 3, 5, 6).reshape(
            occ_groups * vir_groups, occ_local, occupied, vir_local, virtual
        )
        owned = lax.psum_scatter(term, ("occ", "vir"), scatter_dimension=0, tiled=True)[0]
    own_occ = lax.dynamic_slice_in_dim(occ_energy, occ_rank * occ_local, occ_local, 0)
    own_vir = lax.dynamic_slice_in_dim(vir_energy, vir_rank * vir_local, vir_local, 0)
    denom = (
        own_occ[:, None, None, None]
        + occ_energy[None, None, :, None]
        - own_vir[None, :, None, None]
        - vir_energy[None, None, None, :]
    )
    shaped = driver.reshape(occ_local, vir_local, occupied, virtual) + owned.transpose(0, 2, 1, 3)
    return (shaped / denom).reshape(occ_local, vir_local, occupied * virtual)


def solution(mesh):
    return jax.shard_map(
        local,
        mesh=mesh,
        in_specs=(
            P(None, None, ("occ", "vir")),
            P(None, None, ("occ", "vir")),
            P("occ", "vir", None),
            P(),
            P(),
            P(),
            P(),
        ),
        out_specs=P("occ", "vir", None),
        check_vma=False,
    )
```

```python
import functools
import math

import jax
import jax.numpy as jnp
from jax import lax
from jax.experimental import pallas as pl
from jax.experimental.pallas import tpu as pltpu
from jax.sharding import PartitionSpec as P

NV = 768
TILE = 64
LANES = 128
IRREPS = 4
SIZES = (10, 12)
CHUNK = 16


def ladder_kernel(occ_irrep, vir_irrep, place, ycode_ref, *refs, cs, occ_local, steps):
    t_refs, v_refs = refs[:cs], refs[cs:2 * cs]
    out_refs = refs[2 * cs:2 * cs + 4]
    acc, tp, zs, xs, codes, table, slot_of, count = refs[2 * cs + 4:]
    occupied, _, _ = t_refs[0].shape
    virtual = v_refs[0].shape[0]
    tiles = virtual * virtual // LANES
    per_tile = LANES // virtual
    k, g = pl.program_id(0), pl.program_id(1)
    groups = pl.num_programs(1)
    lane = lax.broadcasted_iota(jnp.int32, (occupied, LANES), 1)
    band = 2 * LANES // virtual

    @pl.when((k == 0) & (g == 0))
    def _():
        for x in range(IRREPS):
            count[x] = 0

        @pl.loop(0, table.shape[0])
        def _(s):
            table[s] = 0

        @pl.loop(0, occupied)
        def _(i):
            x = occ_irrep[i]
            s = count[x]
            table[s * IRREPS + x] = i
            slot_of[i] = s
            count[x] = s + 1

        most = jnp.maximum(jnp.maximum(count[0], count[1]), jnp.maximum(count[2], count[3]))
        count[IRREPS] = most
        for label in range(IRREPS):
            codes[label] = jnp.bitwise_xor(ycode_ref[...], label).astype(jnp.float32).astype(jnp.bfloat16)
        codes[IRREPS] = (lane // (LANES // 2)).astype(jnp.float32).astype(jnp.bfloat16)

        @pl.loop(0, most)
        def _(s):
            rows = pl.ds(pl.multiple_of(s * occupied, occupied), occupied)
            for label in range(IRREPS):
                for tile in range(tiles):
                    acc[label, tile, rows, :] = jnp.zeros((occupied, LANES), jnp.float32)

    most = count[IRREPS]
    c_tile = (place[0] + k * cs) // TILE
    c_label = vir_irrep[c_tile]

    first_half = codes[IRREPS] == 0

    def paired(first, second):
        turned = pltpu.roll(second, LANES // 2, second.ndim - 1)
        mask = first_half if first.ndim == 2 else jnp.broadcast_to(first_half[None], first.shape)
        return jnp.where(mask, first, turned), jnp.where(mask, turned, first)

    def work(size, base):
        rows_all = size * occupied
        labels = [jnp.bitwise_xor(c_label, vir_irrep[2 * g + h]) for h in range(2)]
        z = jnp.where(first_half, codes[labels[0]], codes[labels[1]])
        masks = [z == x for x in range(IRREPS - 1)]
        for s in range(size):
            ids = [table[(base + s) * IRREPS + x] for x in range(IRREPS)]
            merged = []
            for c in range(cs):
                out = t_refs[c][ids[IRREPS - 1]]
                for x in range(IRREPS - 1):
                    out = jnp.where(masks[x], t_refs[c][ids[x]], out)
                merged.append(out)
            for p in range(cs // 2):
                halves = paired(merged[2 * p], merged[2 * p + 1])
                for h in range(2):
                    tp[h, p, s * occupied:(s + 1) * occupied, :] = halves[h]
        at = pl.ds(pl.multiple_of(base * occupied, occupied), rows_all)
        for n in range(virtual // band):
            blocks = [v_refs[c][n * band:(n + 1) * band] for c in range(cs)]
            pairs = [paired(blocks[2 * p], blocks[2 * p + 1]) for p in range(cs // 2)]
            for h in range(2):
                weights = jnp.concatenate([pair[h].reshape(2 * LANES, LANES) for pair in pairs], axis=1)
                rows = jnp.concatenate([tp[h, p, :rows_all, :] for p in range(cs // 2)], axis=1)
                part = lax.dot_general(
                    rows, weights, (((1,), (1,)), ((), ())), preferred_element_type=jnp.float32
                )
                acc[labels[h], 2 * n, at, :] += part[:, :LANES]
                acc[labels[h], 2 * n + 1, at, :] += part[:, LANES:]

    low = 0
    for size in SIZES:
        @pl.when((most > low) & (most <= size))
        def _(size=size):
            work(size, 0)
        low = size

    @pl.when(most > low)
    def _():
        @pl.loop(0, (most + CHUNK - 1) // CHUNK)
        def _(r):
            work(CHUNK, r * CHUNK)

    @pl.when((k == steps - 1) & (g == groups - 1))
    def _():
        @pl.loop(0, occupied)
        def _(i):
            x = occ_irrep[i]
            rows = pl.ds(pl.multiple_of(slot_of[i] * occupied, occupied), occupied)
            to = pl.ds(pl.multiple_of(i * occupied, occupied), occupied)
            hit = [ycode_ref[...] == jnp.bitwise_xor(x, label) for label in range(IRREPS - 1)]
            for tile in range(tiles):
                out = acc[IRREPS - 1, tile, rows, :]
                for label in range(IRREPS - 1):
                    out = jnp.where(hit[label], acc[label, tile, rows, :], out)
                xs[tile, to, :] = out

        @pl.loop(0, occupied * occupied // LANES)
        def _(r):
            rows = pl.ds(pl.multiple_of(r * LANES, LANES), LANES)
            for tile in range(tiles):
                zs[tile * LANES:(tile + 1) * LANES, :] = xs[tile, rows, :].T
            for tile in range(tiles):
                mixed = jnp.concatenate(
                    [zs[pl.ds(tile * per_tile + b, virtual, stride=virtual), :] for b in range(per_tile)], axis=0
                )
                acc[0, tile, rows, :] = mixed.T

        near = occ_local // 2
        for part in range(2):
            @pl.loop(0, occupied // occ_local * near)
            def _(r, part=part):
                i = r // near * occ_local + part * near + r % near
                there = jnp.bitwise_xor(r // near, place[1])
                if part == 0 and occupied == 4 * occ_local:
                    there = there % 2 * 2 + there // 2
                to = pl.ds(pl.multiple_of(r % near * occupied, occupied), occupied)
                rows = pl.ds(pl.multiple_of(i * occupied, occupied), occupied)
                for far in range(tiles):
                    tile = jnp.bitwise_xor(place[2], far)
                    value = xs[tile, rows, :] + acc[0, tile, pl.ds(i, occupied, stride=occupied), :]
                    out_refs[2 * part + far % 2][there, far // 2, to, :] = value


def ladder(amplitudes, ladder_integrals, occ_irrep, vir_tile_irrep, first_c, occ_at, vir_at, occ_local):
    occupied, _, cd_local = amplitudes.shape
    virtual = ladder_integrals.shape[0]
    local_c = cd_local // NV
    cs = math.gcd(local_c, TILE, 8)
    assert cs % 2 == 0 and local_c * NV == cd_local and occupied == virtual and LANES % virtual == 0
    groups = NV // LANES
    steps = local_c // cs
    tiles = virtual * virtual // LANES
    place = jnp.stack([first_c, occ_at, vir_at]).astype(jnp.int32)
    ycode = jnp.broadcast_to(occ_irrep[:, None], (occupied, LANES)).astype(jnp.int32)

    def columns(c):
        return pl.BlockSpec((occupied, occupied, LANES), lambda k, g, *_: (0, 0, (k * cs + c) * groups + g))

    piece = jax.ShapeDtypeStruct(
        (occupied // occ_local, tiles // 2, occ_local // 2 * occupied, LANES), jnp.float32
    )
    piece_spec = pl.BlockSpec(piece.shape, lambda k, g, *_: (0, 0, 0, 0))
    slots = -(-occupied // CHUNK) * CHUNK
    return pl.pallas_call(
        functools.partial(ladder_kernel, cs=cs, occ_local=occ_local, steps=steps),
        out_shape=(piece,) * 4,
        grid_spec=pltpu.PrefetchScalarGridSpec(
            num_scalar_prefetch=3,
            grid=(steps, groups),
            in_specs=[pl.BlockSpec((occupied, LANES), lambda k, g, *_: (0, 0))]
            + [columns(c) for c in range(cs)] * 2,
            out_specs=(piece_spec,) * 4,
            scratch_shapes=[
                pltpu.VMEM((IRREPS, tiles, slots * occupied, LANES), jnp.float32),
                pltpu.VMEM((2, cs // 2, CHUNK * occupied, LANES), jnp.bfloat16),
                pltpu.VMEM((tiles * LANES, LANES), jnp.float32),
                pltpu.VMEM((tiles, occupied * occupied, LANES), jnp.float32),
                pltpu.VMEM((IRREPS + 1, occupied, LANES), jnp.bfloat16),
                pltpu.SMEM((slots * IRREPS,), jnp.int32),
                pltpu.SMEM((occupied,), jnp.int32),
                pltpu.SMEM((8,), jnp.int32),
            ],
        ),
        compiler_params=pltpu.CompilerParams(
            dimension_semantics=("arbitrary", "arbitrary"), vmem_limit_bytes=56 * 1024 * 1024
        ),
    )(occ_irrep, vir_tile_irrep, place, ycode, *([amplitudes] * cs), *([ladder_integrals] * cs))


def swap(values, axis, bit):
    size = lax.axis_size(axis)
    return lax.ppermute(values, axis, [(n, n ^ bit) for n in range(size)])


def owned_sum(pieces):
    arrived = [swap(pieces[2 * part + 1], "vir", 1) for part in range(2)]
    order = [(1, 2), (2, 1)]
    kept = [pieces[2 * part] for part in range(2)]
    first = [swap(kept[part][2:] + arrived[part][2:], "occ", order[part][0]) for part in range(2)]
    second = [
        swap(kept[part][1] + arrived[part][1] + first[part][1], "occ", order[part][1]) for part in range(2)
    ]
    mine = jnp.stack(
        [kept[part][0] + arrived[part][0] + first[part][0] + second[part] for part in range(2)], axis=1
    )
    total = mine[0]
    for away in range(1, mine.shape[0]):
        total = total + swap(mine[away], "vir", 2 * away)
    return total


def local(amplitudes, ladder_integrals, driver, occ_energy, vir_energy, occ_irrep, vir_tile_irrep):
    occ_groups = lax.axis_size("occ")
    vir_groups = lax.axis_size("vir")
    occupied = amplitudes.shape[0]
    virtual = ladder_integrals.shape[0]
    occ_local = occupied // occ_groups
    vir_local = virtual // vir_groups
    rank = lax.axis_index(("occ", "vir"))
    occ_rank = lax.axis_index("occ")
    vir_rank = lax.axis_index("vir")
    first_c = rank * (amplitudes.shape[2] // NV)
    tiles = virtual * virtual // LANES
    direct = vir_groups == tiles == 8 and occ_groups == 4
    here = (occ_rank, vir_rank) if direct else (0 * occ_rank, 0 * vir_rank)
    pieces = ladder(amplitudes, ladder_integrals, occ_irrep, vir_tile_irrep, first_c, *here, occ_local)
    if direct:
        owned = owned_sum(pieces).reshape(occ_local, occupied, vir_local, virtual)
    else:
        halves = [jnp.stack([pieces[2 * p], pieces[2 * p + 1]], axis=2) for p in range(2)]
        if occ_groups == 4:
            halves[0] = halves[0][jnp.array([0, 2, 1, 3])]
        term = jnp.stack(halves, axis=3).transpose(1, 2, 0, 3, 4, 5).reshape(
            tiles, occ_groups, occ_local, occupied, vir_groups // tiles, vir_local, virtual
        )
        term = term.transpose(1, 0, 4, 2, 3, 5, 6).reshape(
            occ_groups * vir_groups, occ_local, occupied, vir_local, virtual
        )
        owned = lax.psum_scatter(term, ("occ", "vir"), scatter_dimension=0, tiled=True)[0]
    own_occ = lax.dynamic_slice_in_dim(occ_energy, occ_rank * occ_local, occ_local, 0)
    own_vir = lax.dynamic_slice_in_dim(vir_energy, vir_rank * vir_local, vir_local, 0)
    denom = (
        own_occ[:, None, None, None]
        + occ_energy[None, None, :, None]
        - own_vir[None, :, None, None]
        - vir_energy[None, None, None, :]
    )
    shaped = driver.reshape(occ_local, vir_local, occupied, virtual) + owned.transpose(0, 2, 1, 3)
    return (shaped / denom).reshape(occ_local, vir_local, occupied * virtual)


def solution(mesh):
    return jax.shard_map(
        local,
        mesh=mesh,
        in_specs=(
            P(None, None, ("occ", "vir")),
            P(None, None, ("occ", "vir")),
            P("occ", "vir", None),
            P(),
            P(),
            P(),
            P(),
        ),
        out_specs=P("occ", "vir", None),
        check_vma=False,
    )
```

```python
import functools
import math

import jax
import jax.numpy as jnp
from jax import lax
from jax.experimental import pallas as pl
from jax.experimental.pallas import tpu as pltpu
from jax.sharding import PartitionSpec as P

NV = 768
TILE = 64
LANES = 128
IRREPS = 4
SIZES = (10, 12)
CHUNK = 16


def ladder_kernel(occ_irrep, vir_irrep, place, ycode_ref, *refs, cs, occ_local, steps):
    t_refs, v_refs = refs[:cs], refs[cs:2 * cs]
    out_refs = refs[2 * cs:2 * cs + 4]
    acc, tp, codes, table, slot_of, count = refs[2 * cs + 4:]
    occupied, _, _ = t_refs[0].shape
    virtual = v_refs[0].shape[0]
    tiles = virtual * virtual // LANES
    k, g = pl.program_id(0), pl.program_id(1)
    groups = pl.num_programs(1)
    lane = lax.broadcasted_iota(jnp.int32, (occupied, LANES), 1)
    band = 2 * LANES // virtual

    @pl.when((k == 0) & (g == 0))
    def _():
        for x in range(IRREPS):
            count[x] = 0

        @pl.loop(0, table.shape[0])
        def _(s):
            table[s] = 0

        @pl.loop(0, occupied)
        def _(i):
            x = occ_irrep[i]
            s = count[x]
            table[s * IRREPS + x] = i
            slot_of[i] = s
            count[x] = s + 1

        most = jnp.maximum(jnp.maximum(count[0], count[1]), jnp.maximum(count[2], count[3]))
        count[IRREPS] = most
        for label in range(IRREPS):
            codes[label] = jnp.bitwise_xor(ycode_ref[...], label).astype(jnp.float32).astype(jnp.bfloat16)
        codes[IRREPS] = (lane // (LANES // 2)).astype(jnp.float32).astype(jnp.bfloat16)

        @pl.loop(0, most)
        def _(s):
            rows = pl.ds(pl.multiple_of(s * occupied, occupied), occupied)
            for label in range(IRREPS):
                for tile in range(tiles):
                    acc[label, tile, rows, :] = jnp.zeros((occupied, LANES), jnp.float32)

    most = count[IRREPS]
    c_tile = (place[0] + k * cs) // TILE
    c_label = vir_irrep[c_tile]

    first_half = codes[IRREPS] == 0

    def paired(first, second):
        turned = pltpu.roll(second, LANES // 2, second.ndim - 1)
        mask = first_half if first.ndim == 2 else jnp.broadcast_to(first_half[None], first.shape)
        return jnp.where(mask, first, turned), jnp.where(mask, turned, first)

    def work(size, base):
        rows_all = size * occupied
        labels = [jnp.bitwise_xor(c_label, vir_irrep[2 * g + h]) for h in range(2)]
        z = jnp.where(first_half, codes[labels[0]], codes[labels[1]])
        masks = [z == x for x in range(IRREPS - 1)]
        for s in range(size):
            ids = [table[(base + s) * IRREPS + x] for x in range(IRREPS)]
            merged = []
            for c in range(cs):
                out = t_refs[c][ids[IRREPS - 1]]
                for x in range(IRREPS - 1):
                    out = jnp.where(masks[x], t_refs[c][ids[x]], out)
                merged.append(out)
            for p in range(cs // 2):
                halves = paired(merged[2 * p], merged[2 * p + 1])
                for h in range(2):
                    tp[h, p, s * occupied:(s + 1) * occupied, :] = halves[h]
        at = pl.ds(pl.multiple_of(base * occupied, occupied), rows_all)
        for n in range(virtual // band):
            blocks = [v_refs[c][n * band:(n + 1) * band] for c in range(cs)]
            pairs = [paired(blocks[2 * p], blocks[2 * p + 1]) for p in range(cs // 2)]
            for h in range(2):
                weights = jnp.concatenate([pair[h].reshape(2 * LANES, LANES) for pair in pairs], axis=1)
                rows = jnp.concatenate([tp[h, p, :rows_all, :] for p in range(cs // 2)], axis=1)
                part = lax.dot_general(
                    rows, weights, (((1,), (1,)), ((), ())), preferred_element_type=jnp.float32
                )
                acc[labels[h], 2 * n, at, :] += part[:, :LANES]
                acc[labels[h], 2 * n + 1, at, :] += part[:, LANES:]

    low = 0
    for size in SIZES:
        @pl.when((most > low) & (most <= size))
        def _(size=size):
            work(size, 0)
        low = size

    @pl.when(most > low)
    def _():
        @pl.loop(0, (most + CHUNK - 1) // CHUNK)
        def _(r):
            work(CHUNK, r * CHUNK)

    @pl.when((k == steps - 1) & (g == groups - 1))
    def _():
        near = occ_local // 2
        for part in range(2):
            @pl.loop(0, occupied // occ_local * near)
            def _(r, part=part):
                i = r // near * occ_local + part * near + r % near
                there = jnp.bitwise_xor(r // near, place[1])
                if part == 0 and occupied == 4 * occ_local:
                    there = there % 2 * 2 + there // 2
                x = occ_irrep[i]
                to = pl.ds(pl.multiple_of(r % near * occupied, occupied), occupied)
                rows = pl.ds(pl.multiple_of(slot_of[i] * occupied, occupied), occupied)
                hit = [ycode_ref[...] == jnp.bitwise_xor(x, label) for label in range(IRREPS - 1)]
                for far in range(tiles):
                    tile = jnp.bitwise_xor(place[2], far)
                    value = acc[IRREPS - 1, tile, rows, :]
                    for label in range(IRREPS - 1):
                        value = jnp.where(hit[label], acc[label, tile, rows, :], value)
                    out_refs[2 * part + far % 2][there, far // 2, to, :] = value


def ladder(amplitudes, ladder_integrals, occ_irrep, vir_tile_irrep, first_c, occ_at, vir_at, occ_local):
    occupied, _, cd_local = amplitudes.shape
    virtual = ladder_integrals.shape[0]
    local_c = cd_local // NV
    cs = math.gcd(local_c, TILE, 8)
    assert cs % 2 == 0 and local_c * NV == cd_local and occupied == virtual and LANES % virtual == 0
    groups = NV // LANES
    steps = local_c // cs
    tiles = virtual * virtual // LANES
    place = jnp.stack([first_c, occ_at, vir_at]).astype(jnp.int32)
    ycode = jnp.broadcast_to(occ_irrep[:, None], (occupied, LANES)).astype(jnp.int32)

    def columns(c):
        return pl.BlockSpec((occupied, occupied, LANES), lambda k, g, *_: (0, 0, (k * cs + c) * groups + g))

    piece = jax.ShapeDtypeStruct(
        (occupied // occ_local, tiles // 2, occ_local // 2 * occupied, LANES), jnp.float32
    )
    piece_spec = pl.BlockSpec(piece.shape, lambda k, g, *_: (0, 0, 0, 0))
    slots = -(-occupied // CHUNK) * CHUNK
    return pl.pallas_call(
        functools.partial(ladder_kernel, cs=cs, occ_local=occ_local, steps=steps),
        out_shape=(piece,) * 4,
        grid_spec=pltpu.PrefetchScalarGridSpec(
            num_scalar_prefetch=3,
            grid=(steps, groups),
            in_specs=[pl.BlockSpec((occupied, LANES), lambda k, g, *_: (0, 0))]
            + [columns(c) for c in range(cs)] * 2,
            out_specs=(piece_spec,) * 4,
            scratch_shapes=[
                pltpu.VMEM((IRREPS, tiles, slots * occupied, LANES), jnp.float32),
                pltpu.VMEM((2, cs // 2, CHUNK * occupied, LANES), jnp.bfloat16),
                pltpu.VMEM((IRREPS + 1, occupied, LANES), jnp.bfloat16),
                pltpu.SMEM((slots * IRREPS,), jnp.int32),
                pltpu.SMEM((occupied,), jnp.int32),
                pltpu.SMEM((8,), jnp.int32),
            ],
        ),
        compiler_params=pltpu.CompilerParams(
            dimension_semantics=("arbitrary", "arbitrary"), vmem_limit_bytes=56 * 1024 * 1024
        ),
    )(occ_irrep, vir_tile_irrep, place, ycode, *([amplitudes] * cs), *([ladder_integrals] * cs))


def swap(values, axis, bit):
    size = lax.axis_size(axis)
    return lax.ppermute(values, axis, [(n, n ^ bit) for n in range(size)])


def owned_sum(pieces):
    arrived = [swap(pieces[2 * part + 1], "vir", 1) for part in range(2)]
    order = [(1, 2), (2, 1)]
    kept = [pieces[2 * part] for part in range(2)]
    first = [swap(kept[part][2:] + arrived[part][2:], "occ", order[part][0]) for part in range(2)]
    second = [
        swap(kept[part][1] + arrived[part][1] + first[part][1], "occ", order[part][1]) for part in range(2)
    ]
    mine = jnp.stack(
        [kept[part][0] + arrived[part][0] + first[part][0] + second[part] for part in range(2)], axis=1
    )
    total = mine[0]
    for away in range(1, mine.shape[0]):
        total = total + swap(mine[away], "vir", 2 * away)
    return total


def local(amplitudes, ladder_integrals, driver, occ_energy, vir_energy, occ_irrep, vir_tile_irrep):
    occ_groups = lax.axis_size("occ")
    vir_groups = lax.axis_size("vir")
    occupied = amplitudes.shape[0]
    virtual = ladder_integrals.shape[0]
    occ_local = occupied // occ_groups
    vir_local = virtual // vir_groups
    rank = lax.axis_index(("occ", "vir"))
    occ_rank = lax.axis_index("occ")
    vir_rank = lax.axis_index("vir")
    first_c = rank * (amplitudes.shape[2] // NV)
    tiles = virtual * virtual // LANES
    direct = vir_groups == tiles == 8 and occ_groups == 4
    here = (occ_rank, vir_rank) if direct else (0 * occ_rank, 0 * vir_rank)
    pieces = ladder(amplitudes, ladder_integrals, occ_irrep, vir_tile_irrep, first_c, *here, occ_local)
    if direct:
        owned = owned_sum(pieces).reshape(occ_local, occupied, vir_local, virtual)
    else:
        halves = [jnp.stack([pieces[2 * p], pieces[2 * p + 1]], axis=2) for p in range(2)]
        if occ_groups == 4:
            halves[0] = halves[0][jnp.array([0, 2, 1, 3])]
        term = jnp.stack(halves, axis=3).transpose(1, 2, 0, 3, 4, 5).reshape(
            tiles, occ_groups, occ_local, occupied, vir_groups // tiles, vir_local, virtual
        )
        term = term.transpose(1, 0, 4, 2, 3, 5, 6).reshape(
            occ_groups * vir_groups, occ_local, occupied, vir_local, virtual
        )
        owned = lax.psum_scatter(term, ("occ", "vir"), scatter_dimension=0, tiled=True)[0]
    own_occ = lax.dynamic_slice_in_dim(occ_energy, occ_rank * occ_local, occ_local, 0)
    own_vir = lax.dynamic_slice_in_dim(vir_energy, vir_rank * vir_local, vir_local, 0)
    denom = (
        own_occ[:, None, None, None]
        + occ_energy[None, None, :, None]
        - own_vir[None, :, None, None]
        - vir_energy[None, None, None, :]
    )
    blocks = owned.reshape(occ_local, occ_groups, occ_local, vir_local, vir_groups, vir_local)
    blocks = blocks.transpose(1, 4, 2, 5, 0, 3).reshape(occ_groups * vir_groups, (occ_local * vir_local) ** 2)
    mirror = lax.all_to_all(blocks, ("occ", "vir"), 0, 0, tiled=True)
    mirror = mirror.reshape(occ_groups, vir_groups, occ_local, vir_local, occ_local, vir_local)
    mirror = mirror.transpose(2, 3, 0, 4, 1, 5).reshape(occ_local, vir_local, occupied, virtual)
    shaped = driver.reshape(occ_local, vir_local, occupied, virtual) + (owned.transpose(0, 2, 1, 3) + mirror)
    return (shaped / denom).reshape(occ_local, vir_local, occupied * virtual)


def solution(mesh):
    return jax.shard_map(
        local,
        mesh=mesh,
        in_specs=(
            P(None, None, ("occ", "vir")),
            P(None, None, ("occ", "vir")),
            P("occ", "vir", None),
            P(),
            P(),
            P(),
            P(),
        ),
        out_specs=P("occ", "vir", None),
        check_vma=False,
    )
```

```python
import functools
import math

import jax
import jax.numpy as jnp
from jax import lax
from jax.experimental import pallas as pl
from jax.experimental.pallas import tpu as pltpu
from jax.sharding import PartitionSpec as P

NV = 768
TILE = 64
LANES = 128
SPOTS = 4
WIDTH = SPOTS * TILE
IRREPS = 4
SIZES = (10, 12)
CHUNK = 8


def ladder_kernel(occ_irrep, vir_irrep, place, ycode_ref, *refs, cs, occ_local, steps):
    t_refs, v_refs = refs[:cs], refs[cs:2 * cs]
    out_refs = refs[2 * cs:2 * cs + 4]
    acc, tp, zs, xs, codes, table, slot_of, count = refs[2 * cs + 4:]
    occupied, _, _ = t_refs[0].shape
    virtual = v_refs[0].shape[0]
    tiles = virtual * virtual // LANES
    per_tile = LANES // virtual
    k, g = pl.program_id(0), pl.program_id(1)
    groups = pl.num_programs(1)
    lane = lax.broadcasted_iota(jnp.int32, (occupied, WIDTH), 1)
    band = 2 * LANES // virtual

    @pl.when((k == 0) & (g == 0))
    def _():
        for x in range(IRREPS):
            count[x] = 0

        @pl.loop(0, table.shape[0])
        def _(s):
            table[s] = 0

        @pl.loop(0, occupied)
        def _(i):
            x = occ_irrep[i]
            s = count[x]
            table[s * IRREPS + x] = i
            slot_of[i] = s
            count[x] = s + 1

        most = jnp.maximum(jnp.maximum(count[0], count[1]), jnp.maximum(count[2], count[3]))
        count[IRREPS] = most
        for label in range(IRREPS):
            code = jnp.bitwise_xor(ycode_ref[...], label).astype(jnp.float32).astype(jnp.bfloat16)
            codes[label] = jnp.concatenate([code, code], axis=1)
        codes[IRREPS] = (lane // TILE).astype(jnp.float32).astype(jnp.bfloat16)

        @pl.loop(0, most)
        def _(s):
            rows = pl.ds(pl.multiple_of(s * occupied, occupied), occupied)
            for label in range(IRREPS):
                for tile in range(tiles):
                    acc[label, tile, rows, :] = jnp.zeros((occupied, LANES), jnp.float32)

    most = count[IRREPS]
    c_tile = (place[0] + k * cs) // TILE
    c_label = vir_irrep[c_tile]

    spot = codes[IRREPS]
    here = [spot == t for t in range(SPOTS)]
    turned = pltpu.roll(spot, TILE, 1)
    there = [turned == (t - 1) % SPOTS for t in range(SPOTS)]

    def gathered(blocks):
        blocks = blocks + [jnp.zeros_like(blocks[0])] * (SPOTS - len(blocks))
        axis = blocks[0].ndim - 1
        moved = [block if c == 0 else pltpu.roll(block, c * TILE, axis) for c, block in enumerate(blocks)]
        masks = [mask if axis == 1 else jnp.broadcast_to(mask[None], blocks[0].shape) for mask in there]
        out = []
        for d in range(SPOTS):
            value = moved[SPOTS - 1]
            for c in range(SPOTS - 1):
                value = jnp.where(masks[(d + c) % SPOTS], moved[c], value)
            out.append(value)
        return out

    def work(size, base):
        labels = [jnp.bitwise_xor(c_label, vir_irrep[SPOTS * g + d]) for d in range(SPOTS)]
        z = codes[labels[SPOTS - 1]]
        for d in range(SPOTS - 1):
            z = jnp.where(here[d], codes[labels[d]], z)
        masks = [z == x for x in range(IRREPS - 1)]
        for s in range(size):
            ids = [table[(base + s) * IRREPS + x] for x in range(IRREPS)]
            merged = []
            for c in range(cs):
                out = t_refs[c][ids[IRREPS - 1]]
                for x in range(IRREPS - 1):
                    out = jnp.where(masks[x], t_refs[c][ids[x]], out)
                merged.append(out)
            for f in range(0, cs, SPOTS):
                lanes = slice(f // SPOTS * WIDTH, (f // SPOTS + 1) * WIDTH)
                for d, value in enumerate(gathered(merged[f:f + SPOTS])):
                    tp[d, s * occupied:(s + 1) * occupied, lanes] = value
        at = pl.ds(pl.multiple_of(base * occupied, occupied), size * occupied)
        for n in range(virtual // band):
            groups_of = [
                gathered([v_refs[c][n * band:(n + 1) * band] for c in range(f, min(f + SPOTS, cs))])
                for f in range(0, cs, SPOTS)
            ]
            for d in range(SPOTS):
                weights = jnp.concatenate([part[d].reshape(2 * LANES, WIDTH) for part in groups_of], axis=1)
                part = lax.dot_general(
                    tp[d, :size * occupied, :], weights, (((1,), (1,)), ((), ())),
                    preferred_element_type=jnp.float32,
                )
                acc[labels[d], 2 * n, at, :] += part[:, :LANES]
                acc[labels[d], 2 * n + 1, at, :] += part[:, LANES:]

    low = 0
    for size in SIZES:
        @pl.when((most > low) & (most <= size))
        def _(size=size):
            work(size, 0)
        low = size

    @pl.when(most > low)
    def _():
        @pl.loop(0, (most + CHUNK - 1) // CHUNK)
        def _(r):
            work(CHUNK, r * CHUNK)

    @pl.when((k == steps - 1) & (g == groups - 1))
    def _():
        @pl.loop(0, occupied)
        def _(i):
            x = occ_irrep[i]
            rows = pl.ds(pl.multiple_of(slot_of[i] * occupied, occupied), occupied)
            to = pl.ds(pl.multiple_of(i * occupied, occupied), occupied)
            hit = [ycode_ref[...] == jnp.bitwise_xor(x, label) for label in range(IRREPS - 1)]
            for tile in range(tiles):
                out = acc[IRREPS - 1, tile, rows, :]
                for label in range(IRREPS - 1):
                    out = jnp.where(hit[label], acc[label, tile, rows, :], out)
                xs[tile, to, :] = out

        @pl.loop(0, occupied * occupied // LANES)
        def _(r):
            rows = pl.ds(pl.multiple_of(r * LANES, LANES), LANES)
            for tile in range(tiles):
                zs[tile * LANES:(tile + 1) * LANES, :] = xs[tile, rows, :].T
            for tile in range(tiles):
                mixed = jnp.concatenate(
                    [zs[pl.ds(tile * per_tile + b, virtual, stride=virtual), :] for b in range(per_tile)], axis=0
                )
                acc[0, tile, rows, :] = mixed.T

        near = occ_local // 2
        for part in range(2):
            @pl.loop(0, occupied // occ_local * near)
            def _(r, part=part):
                i = r // near * occ_local + part * near + r % near
                there = jnp.bitwise_xor(r // near, place[1])
                if part == 0 and occupied == 4 * occ_local:
                    there = there % 2 * 2 + there // 2
                to = pl.ds(pl.multiple_of(r % near * occupied, occupied), occupied)
                rows = pl.ds(pl.multiple_of(i * occupied, occupied), occupied)
                for far in range(tiles):
                    tile = jnp.bitwise_xor(place[2], far)
                    value = xs[tile, rows, :] + acc[0, tile, pl.ds(i, occupied, stride=occupied), :]
                    out_refs[2 * part + far % 2][there, far // 2, to, :] = value


def ladder(amplitudes, ladder_integrals, occ_irrep, vir_tile_irrep, first_c, occ_at, vir_at, occ_local):
    occupied, _, cd_local = amplitudes.shape
    virtual = ladder_integrals.shape[0]
    local_c = cd_local // NV
    cs = math.gcd(local_c, TILE, 4)
    assert cs % 2 == 0 and local_c * NV == cd_local and occupied == virtual and LANES % virtual == 0
    groups = NV // WIDTH
    steps = local_c // cs
    tiles = virtual * virtual // LANES
    place = jnp.stack([first_c, occ_at, vir_at]).astype(jnp.int32)
    ycode = jnp.broadcast_to(occ_irrep[:, None], (occupied, LANES)).astype(jnp.int32)

    def columns(c):
        return pl.BlockSpec((occupied, occupied, WIDTH), lambda k, g, *_: (0, 0, (k * cs + c) * groups + g))

    piece = jax.ShapeDtypeStruct(
        (occupied // occ_local, tiles // 2, occ_local // 2 * occupied, LANES), jnp.float32
    )
    piece_spec = pl.BlockSpec(piece.shape, lambda k, g, *_: (0, 0, 0, 0))
    slots = -(-occupied // CHUNK) * CHUNK
    return pl.pallas_call(
        functools.partial(ladder_kernel, cs=cs, occ_local=occ_local, steps=steps),
        out_shape=(piece,) * 4,
        grid_spec=pltpu.PrefetchScalarGridSpec(
            num_scalar_prefetch=3,
            grid=(steps, groups),
            in_specs=[pl.BlockSpec((occupied, LANES), lambda k, g, *_: (0, 0))]
            + [columns(c) for c in range(cs)] * 2,
            out_specs=(piece_spec,) * 4,
            scratch_shapes=[
                pltpu.VMEM((IRREPS, tiles, slots * occupied, LANES), jnp.float32),
                pltpu.VMEM((SPOTS, max(SIZES + (CHUNK,)) * occupied, -(-cs // SPOTS) * WIDTH), jnp.bfloat16),
                pltpu.VMEM((tiles * LANES, LANES), jnp.float32),
                pltpu.VMEM((tiles, occupied * occupied, LANES), jnp.float32),
                pltpu.VMEM((IRREPS + 1, occupied, WIDTH), jnp.bfloat16),
                pltpu.SMEM((slots * IRREPS,), jnp.int32),
                pltpu.SMEM((occupied,), jnp.int32),
                pltpu.SMEM((8,), jnp.int32),
            ],
        ),
        compiler_params=pltpu.CompilerParams(
            dimension_semantics=("arbitrary", "arbitrary"), vmem_limit_bytes=56 * 1024 * 1024
        ),
    )(occ_irrep, vir_tile_irrep, place, ycode, *([amplitudes] * cs), *([ladder_integrals] * cs))


def swap(values, axis, bit):
    size = lax.axis_size(axis)
    return lax.ppermute(values, axis, [(n, n ^ bit) for n in range(size)])


def owned_sum(pieces):
    arrived = [swap(pieces[2 * part + 1], "vir", 1) for part in range(2)]
    order = [(1, 2), (2, 1)]
    kept = [pieces[2 * part] for part in range(2)]
    first = [swap(kept[part][2:] + arrived[part][2:], "occ", order[part][0]) for part in range(2)]
    second = [
        swap(kept[part][1] + arrived[part][1] + first[part][1], "occ", order[part][1]) for part in range(2)
    ]
    mine = jnp.stack(
        [kept[part][0] + arrived[part][0] + first[part][0] + second[part] for part in range(2)], axis=1
    )
    total = mine[0]
    for away in range(1, mine.shape[0]):
        total = total + swap(mine[away], "vir", 2 * away)
    return total


def local(amplitudes, ladder_integrals, driver, occ_energy, vir_energy, occ_irrep, vir_tile_irrep):
    occ_groups = lax.axis_size("occ")
    vir_groups = lax.axis_size("vir")
    occupied = amplitudes.shape[0]
    virtual = ladder_integrals.shape[0]
    occ_local = occupied // occ_groups
    vir_local = virtual // vir_groups
    rank = lax.axis_index(("occ", "vir"))
    occ_rank = lax.axis_index("occ")
    vir_rank = lax.axis_index("vir")
    first_c = rank * (amplitudes.shape[2] // NV)
    tiles = virtual * virtual // LANES
    direct = vir_groups == tiles == 8 and occ_groups == 4
    here = (occ_rank, vir_rank) if direct else (0 * occ_rank, 0 * vir_rank)
    pieces = ladder(amplitudes, ladder_integrals, occ_irrep, vir_tile_irrep, first_c, *here, occ_local)
    if direct:
        owned = owned_sum(pieces).reshape(occ_local, occupied, vir_local, virtual)
    else:
        halves = [jnp.stack([pieces[2 * p], pieces[2 * p + 1]], axis=2) for p in range(2)]
        if occ_groups == 4:
            halves[0] = halves[0][jnp.array([0, 2, 1, 3])]
        term = jnp.stack(halves, axis=3).transpose(1, 2, 0, 3, 4, 5).reshape(
            tiles, occ_groups, occ_local, occupied, vir_groups // tiles, vir_local, virtual
        )
        term = term.transpose(1, 0, 4, 2, 3, 5, 6).reshape(
            occ_groups * vir_groups, occ_local, occupied, vir_local, virtual
        )
        owned = lax.psum_scatter(term, ("occ", "vir"), scatter_dimension=0, tiled=True)[0]
    own_occ = lax.dynamic_slice_in_dim(occ_energy, occ_rank * occ_local, occ_local, 0)
    own_vir = lax.dynamic_slice_in_dim(vir_energy, vir_rank * vir_local, vir_local, 0)
    denom = (
        own_occ[:, None, None, None]
        + occ_energy[None, None, :, None]
        - own_vir[None, :, None, None]
        - vir_energy[None, None, None, :]
    )
    shaped = driver.reshape(occ_local, vir_local, occupied, virtual) + owned.transpose(0, 2, 1, 3)
    return (shaped / denom).reshape(occ_local, vir_local, occupied * virtual)


def solution(mesh):
    return jax.shard_map(
        local,
        mesh=mesh,
        in_specs=(
            P(None, None, ("occ", "vir")),
            P(None, None, ("occ", "vir")),
            P("occ", "vir", None),
            P(),
            P(),
            P(),
            P(),
        ),
        out_specs=P("occ", "vir", None),
        check_vma=False,
    )
```

```python
import functools
import math

import jax
import jax.numpy as jnp
from jax import lax
from jax.experimental import pallas as pl
from jax.experimental.pallas import tpu as pltpu
from jax.sharding import PartitionSpec as P

NV = 768
TILE = 64
LANES = 128
IRREPS = 4
SIZES = (12,)
CHUNK = 16


def ladder_kernel(occ_irrep, vir_irrep, place, ycode_ref, ylane_ref, *refs, cs, occ_local, steps):
    t_refs, v_refs = refs[:cs], refs[cs:2 * cs]
    out_refs = refs[2 * cs:2 * cs + 4]
    acc, tp, xt, picked, codes, table, slot_of, count = refs[2 * cs + 4:]
    occupied, _, _ = t_refs[0].shape
    virtual = v_refs[0].shape[0]
    pairs_all = virtual * virtual
    tiles = pairs_all // LANES
    per_tile = LANES // occupied
    k, g = pl.program_id(0), pl.program_id(1)
    groups = pl.num_programs(1)
    lane = lax.broadcasted_iota(jnp.int32, (occupied, LANES), 1)

    @pl.when((k == 0) & (g == 0))
    def _():
        for x in range(IRREPS):
            count[x] = 0

        @pl.loop(0, table.shape[0])
        def _(s):
            table[s] = 0

        @pl.loop(0, occupied)
        def _(i):
            x = occ_irrep[i]
            s = count[x]
            table[s * IRREPS + x] = i
            slot_of[i] = s
            count[x] = s + 1

        most = jnp.maximum(jnp.maximum(count[0], count[1]), jnp.maximum(count[2], count[3]))
        count[IRREPS] = most
        for label in range(IRREPS):
            codes[label] = jnp.bitwise_xor(ycode_ref[...], label).astype(jnp.float32).astype(jnp.bfloat16)
        codes[IRREPS] = (lane // (LANES // 2)).astype(jnp.float32).astype(jnp.bfloat16)

        @pl.loop(0, (most + per_tile - 1) // per_tile)
        def _(t):
            for label in range(IRREPS):
                acc[label, t] = jnp.zeros((pairs_all, LANES), jnp.float32)

    most = count[IRREPS]
    c_tile = (place[0] + k * cs) // TILE
    c_label = vir_irrep[c_tile]

    first_half = pltpu.roll(codes[IRREPS], LANES // 2, 1) == 1

    def paired(first, second):
        turned = pltpu.roll(second, LANES // 2, second.ndim - 1)
        mask = first_half if first.ndim == 2 else jnp.broadcast_to(first_half[None], first.shape)
        return jnp.where(mask, first, turned), jnp.where(mask, turned, first)

    def work(size, base):
        rows_all = size * occupied
        labels = [jnp.bitwise_xor(c_label, vir_irrep[2 * g + h]) for h in range(2)]
        z = jnp.where(codes[IRREPS] == 0, codes[labels[0]], codes[labels[1]])
        masks = [z == x for x in range(IRREPS - 1)]
        for s in range(size):
            ids = [table[(base + s) * IRREPS + x] for x in range(IRREPS)]
            merged = []
            for c in range(cs):
                out = t_refs[c][ids[IRREPS - 1]]
                for x in range(IRREPS - 1):
                    out = jnp.where(masks[x], t_refs[c][ids[x]], out)
                merged.append(out)
            for p in range(cs // 2):
                halves = paired(merged[2 * p], merged[2 * p + 1])
                for h in range(2):
                    tp[h, s * occupied:(s + 1) * occupied, p * LANES:(p + 1) * LANES] = halves[h]
        pairs = [paired(v_refs[2 * p][...], v_refs[2 * p + 1][...]) for p in range(cs // 2)]
        for h in range(2):
            stream = jnp.concatenate([pair[h].reshape(pairs_all, LANES) for pair in pairs], axis=1)
            part = lax.dot_general(
                stream, tp[h, :rows_all, :], (((1,), (1,)), ((), ())), preferred_element_type=jnp.float32
            )
            for t in range(size // per_tile):
                acc[labels[h], base // per_tile + t] += part[:, t * LANES:(t + 1) * LANES]

    low = 0
    for size in SIZES:
        @pl.when((most > low) & (most <= size))
        def _(size=size):
            work(size, 0)
        low = size

    @pl.when(most > low)
    def _():
        @pl.loop(0, (most + CHUNK - 1) // CHUNK)
        def _(r):
            work(CHUNK, r * CHUNK)

    @pl.when((k == steps - 1) & (g == groups - 1))
    def _():
        slot_tiles = (most + per_tile - 1) // per_tile
        group = lax.broadcasted_iota(jnp.int32, (LANES, LANES), 1) // occupied
        lane_irrep = jnp.broadcast_to(ylane_ref[0:1, :], (LANES, LANES))

        @pl.loop(0, tiles)
        def _(r):
            rows = pl.ds(pl.multiple_of(r * LANES, LANES), LANES)

            @pl.loop(0, slot_tiles)
            def _(t):
                sums = [acc[label, t, rows, :] for label in range(IRREPS)]
                for x in range(IRREPS):
                    value = sums[IRREPS - 1]
                    for label in range(IRREPS - 1):
                        value = jnp.where(lane_irrep == label ^ x, sums[label], value)
                    picked[x, t] = value

            @pl.loop(0, tiles)
            def _(it):
                value = None
                for u in range(per_tile):
                    i = it * per_tile + u
                    slot = slot_of[i]
                    shift = (u - slot % per_tile + per_tile) % per_tile * occupied
                    turned = pltpu.roll(picked[occ_irrep[i], slot // per_tile], shift, 1)
                    value = turned if value is None else jnp.where(group == u, turned, value)
                xt[it, rows, :] = value

        def strided(load, first):
            return jnp.concatenate([load(first + u) for u in range(per_tile)], axis=0)

        @pl.loop(0, tiles)
        def _(r):
            for jt in range(tiles):
                swapped = strided(lambda a: xt[jt, pl.ds(a, virtual, stride=virtual), :], r * per_tile)
                acc[0, r, jt * LANES:(jt + 1) * LANES, :] = swapped.T

        @pl.loop(0, tiles // 2)
        def _(f):
            for core in range(2):
                tile = jnp.bitwise_xor(2 * f + core, place[2])
                rows = pl.ds(pl.multiple_of(tile * LANES, LANES), LANES)
                for it in range(tiles):
                    there = jnp.bitwise_xor(it // 2, place[1])
                    if it % 2 == 0 and occupied == 4 * occ_local:
                        there = there % 2 * 2 + there // 2
                    swapped = strided(lambda i: acc[0, tile, pl.ds(i, occupied, stride=occupied), :], it * per_tile)
                    out_refs[2 * (it % 2) + core][there, f] = xt[it, rows, :].T + swapped


def ladder(amplitudes, ladder_integrals, occ_irrep, vir_tile_irrep, first_c, occ_at, vir_at, occ_local):
    occupied, _, cd_local = amplitudes.shape
    virtual = ladder_integrals.shape[0]
    local_c = cd_local // NV
    cs = math.gcd(local_c, TILE, 8)
    assert cs % 2 == 0 and local_c * NV == cd_local and occupied == virtual and LANES % virtual == 0
    groups = NV // LANES
    steps = local_c // cs
    tiles = virtual * virtual // LANES
    place = jnp.stack([first_c, occ_at, vir_at]).astype(jnp.int32)
    assert occ_local // 2 * occupied == LANES
    ycode = jnp.broadcast_to(occ_irrep[:, None], (occupied, LANES)).astype(jnp.int32)
    ylane = jnp.broadcast_to(jnp.tile(occ_irrep, LANES // occupied)[None], (8, LANES)).astype(jnp.int32)

    def columns(c):
        return pl.BlockSpec((occupied, occupied, LANES), lambda k, g, *_: (0, 0, (k * cs + c) * groups + g))

    piece = jax.ShapeDtypeStruct(
        (occupied // occ_local, tiles // 2, occ_local // 2 * occupied, LANES), jnp.float32
    )
    piece_spec = pl.BlockSpec(piece.shape, lambda k, g, *_: (0, 0, 0, 0))
    slots = -(-occupied // CHUNK) * CHUNK
    return pl.pallas_call(
        functools.partial(ladder_kernel, cs=cs, occ_local=occ_local, steps=steps),
        out_shape=(piece,) * 4,
        grid_spec=pltpu.PrefetchScalarGridSpec(
            num_scalar_prefetch=3,
            grid=(steps, groups),
            in_specs=[pl.BlockSpec((occupied, LANES), lambda k, g, *_: (0, 0))]
            + [pl.BlockSpec((8, LANES), lambda k, g, *_: (0, 0))]
            + [columns(c) for c in range(cs)] * 2,
            out_specs=(piece_spec,) * 4,
            scratch_shapes=[
                pltpu.VMEM((IRREPS, slots * occupied // LANES, virtual * virtual, LANES), jnp.float32),
                pltpu.VMEM((2, CHUNK * occupied, cs // 2 * LANES), jnp.bfloat16),
                pltpu.VMEM((tiles, virtual * virtual, LANES), jnp.float32),
                pltpu.VMEM((IRREPS, slots * occupied // LANES, LANES, LANES), jnp.float32),
                pltpu.VMEM((IRREPS + 1, occupied, LANES), jnp.bfloat16),
                pltpu.SMEM((slots * IRREPS,), jnp.int32),
                pltpu.SMEM((occupied,), jnp.int32),
                pltpu.SMEM((8,), jnp.int32),
            ],
        ),
        compiler_params=pltpu.CompilerParams(
            dimension_semantics=("arbitrary", "arbitrary"), vmem_limit_bytes=56 * 1024 * 1024
        ),
    )(occ_irrep, vir_tile_irrep, place, ycode, ylane, *([amplitudes] * cs), *([ladder_integrals] * cs))


def swap(values, axis, bit):
    size = lax.axis_size(axis)
    return lax.ppermute(values, axis, [(n, n ^ bit) for n in range(size)])


def owned_sum(pieces):
    arrived = [swap(pieces[2 * part + 1], "vir", 1) for part in range(2)]
    order = [(1, 2), (2, 1)]
    kept = [pieces[2 * part] for part in range(2)]
    first = [swap(kept[part][2:] + arrived[part][2:], "occ", order[part][0]) for part in range(2)]
    second = [
        swap(kept[part][1] + arrived[part][1] + first[part][1], "occ", order[part][1]) for part in range(2)
    ]
    mine = jnp.stack(
        [kept[part][0] + arrived[part][0] + first[part][0] + second[part] for part in range(2)], axis=1
    )
    total = mine[0]
    for away in range(1, mine.shape[0]):
        total = total + swap(mine[away], "vir", 2 * away)
    return total


def local(amplitudes, ladder_integrals, driver, occ_energy, vir_energy, occ_irrep, vir_tile_irrep):
    occ_groups = lax.axis_size("occ")
    vir_groups = lax.axis_size("vir")
    occupied = amplitudes.shape[0]
    virtual = ladder_integrals.shape[0]
    occ_local = occupied // occ_groups
    vir_local = virtual // vir_groups
    rank = lax.axis_index(("occ", "vir"))
    occ_rank = lax.axis_index("occ")
    vir_rank = lax.axis_index("vir")
    first_c = rank * (amplitudes.shape[2] // NV)
    tiles = virtual * virtual // LANES
    direct = vir_groups == tiles == 8 and occ_groups == 4
    here = (occ_rank, vir_rank) if direct else (0 * occ_rank, 0 * vir_rank)
    pieces = ladder(amplitudes, ladder_integrals, occ_irrep, vir_tile_irrep, first_c, *here, occ_local)
    if direct:
        owned = owned_sum(pieces).reshape(occ_local, occupied, vir_local, virtual)
    else:
        halves = [jnp.stack([pieces[2 * p], pieces[2 * p + 1]], axis=2) for p in range(2)]
        if occ_groups == 4:
            halves[0] = halves[0][jnp.array([0, 2, 1, 3])]
        term = jnp.stack(halves, axis=3).transpose(1, 2, 0, 3, 4, 5).reshape(
            tiles, occ_groups, occ_local, occupied, vir_groups // tiles, vir_local, virtual
        )
        term = term.transpose(1, 0, 4, 2, 3, 5, 6).reshape(
            occ_groups * vir_groups, occ_local, occupied, vir_local, virtual
        )
        owned = lax.psum_scatter(term, ("occ", "vir"), scatter_dimension=0, tiled=True)[0]
    own_occ = lax.dynamic_slice_in_dim(occ_energy, occ_rank * occ_local, occ_local, 0)
    own_vir = lax.dynamic_slice_in_dim(vir_energy, vir_rank * vir_local, vir_local, 0)
    denom = (
        own_occ[:, None, None, None]
        + occ_energy[None, None, :, None]
        - own_vir[None, :, None, None]
        - vir_energy[None, None, None, :]
    )
    shaped = driver.reshape(occ_local, vir_local, occupied, virtual) + owned.transpose(0, 2, 1, 3)
    return (shaped / denom).reshape(occ_local, vir_local, occupied * virtual)


def solution(mesh):
    return jax.shard_map(
        local,
        mesh=mesh,
        in_specs=(
            P(None, None, ("occ", "vir")),
            P(None, None, ("occ", "vir")),
            P("occ", "vir", None),
            P(),
            P(),
            P(),
            P(),
        ),
        out_specs=P("occ", "vir", None),
        check_vma=False,
    )
```

```python
import functools
import math

import jax
import jax.numpy as jnp
from jax import lax
from jax.experimental import pallas as pl
from jax.experimental.pallas import tpu as pltpu
from jax.sharding import PartitionSpec as P

NV = 768
TILE = 64
LANES = 128
IRREPS = 4
SIZES = (10, 12)
CHUNK = 16


def ladder_kernel(occ_irrep, vir_irrep, place, ycode_ref, *refs, cs, occ_local, steps):
    t_refs, v_refs = refs[:cs], refs[cs:2 * cs]
    out_refs = refs[2 * cs:2 * cs + 6]
    acc, tp, zs, xs, codes, table, slot_of, count = refs[2 * cs + 6:]
    occupied, _, _ = t_refs[0].shape
    virtual = v_refs[0].shape[0]
    tiles = virtual * virtual // LANES
    per_tile = LANES // virtual
    k, g = pl.program_id(0), pl.program_id(1)
    groups = pl.num_programs(1)
    lane = lax.broadcasted_iota(jnp.int32, (occupied, LANES), 1)
    band = 4 * LANES // virtual

    @pl.when((k == 0) & (g == 0))
    def _():
        for x in range(IRREPS):
            count[x] = 0

        @pl.loop(0, table.shape[0])
        def _(s):
            table[s] = 0

        @pl.loop(0, occupied)
        def _(i):
            x = occ_irrep[i]
            s = count[x]
            table[s * IRREPS + x] = i
            slot_of[i] = s
            count[x] = s + 1

        most = jnp.maximum(jnp.maximum(count[0], count[1]), jnp.maximum(count[2], count[3]))
        count[IRREPS] = most
        for label in range(IRREPS):
            codes[label] = jnp.bitwise_xor(ycode_ref[...], label).astype(jnp.float32).astype(jnp.bfloat16)
        codes[IRREPS] = (lane // (LANES // 2)).astype(jnp.float32).astype(jnp.bfloat16)

        @pl.loop(0, most)
        def _(s):
            rows = pl.ds(pl.multiple_of(s * occupied, occupied), occupied)
            for label in range(IRREPS):
                for tile in range(tiles):
                    acc[label, tile, rows, :] = jnp.zeros((occupied, LANES), jnp.float32)

    most = count[IRREPS]
    c_tile = (place[0] + k * cs) // TILE
    c_label = vir_irrep[c_tile]

    first_half = codes[IRREPS] == 0

    def work(size, base):
        rows_all = size * occupied
        labels = [jnp.bitwise_xor(c_label, vir_irrep[2 * g + h]) for h in range(2)]
        z = jnp.where(first_half, codes[labels[0]], codes[labels[1]])
        masks = [z == x for x in range(IRREPS - 1)]
        nothing = jnp.zeros((occupied, LANES), jnp.bfloat16)
        for s in range(size):
            ids = [table[(base + s) * IRREPS + x] for x in range(IRREPS)]
            for c in range(cs):
                out = t_refs[c][ids[IRREPS - 1]]
                for x in range(IRREPS - 1):
                    out = jnp.where(masks[x], t_refs[c][ids[x]], out)
                lanes = slice(c * LANES, (c + 1) * LANES)
                tp[s * occupied:(s + 1) * occupied, lanes] = jnp.where(first_half, out, nothing)
                tp[rows_all + s * occupied:rows_all + (s + 1) * occupied, lanes] = jnp.where(first_half, nothing, out)
        at = pl.ds(pl.multiple_of(base * occupied, occupied), rows_all)
        for n in range(virtual // band):
            weights = jnp.concatenate(
                [v_refs[c][n * band:(n + 1) * band].reshape(band * virtual, LANES) for c in range(cs)], axis=1
            )
            part = lax.dot_general(
                tp[:2 * rows_all, :], weights, (((1,), (1,)), ((), ())), preferred_element_type=jnp.float32
            )
            for h in range(2):
                for t in range(band * virtual // LANES):
                    acc[labels[h], band * virtual // LANES * n + t, at, :] += part[
                        h * rows_all:(h + 1) * rows_all, t * LANES:(t + 1) * LANES
                    ]

    low = 0
    for size in SIZES:
        @pl.when((most > low) & (most <= size))
        def _(size=size):
            work(size, 0)
        low = size

    @pl.when(most > low)
    def _():
        @pl.loop(0, (most + CHUNK - 1) // CHUNK)
        def _(r):
            work(CHUNK, r * CHUNK)

    @pl.when((k == steps - 1) & (g == groups - 1))
    def _():
        @pl.loop(0, occupied)
        def _(i):
            x = occ_irrep[i]
            rows = pl.ds(pl.multiple_of(slot_of[i] * occupied, occupied), occupied)
            to = pl.ds(pl.multiple_of(i * occupied, occupied), occupied)
            hit = [ycode_ref[...] == jnp.bitwise_xor(x, label) for label in range(IRREPS - 1)]
            for tile in range(tiles):
                out = acc[IRREPS - 1, tile, rows, :]
                for label in range(IRREPS - 1):
                    out = jnp.where(hit[label], acc[label, tile, rows, :], out)
                xs[tile, to, :] = out

        @pl.loop(0, occupied * occupied // LANES)
        def _(r):
            rows = pl.ds(pl.multiple_of(r * LANES, LANES), LANES)
            for tile in range(tiles):
                zs[tile * LANES:(tile + 1) * LANES, :] = xs[tile, rows, :].T
            for tile in range(tiles):
                mixed = jnp.concatenate(
                    [zs[pl.ds(tile * per_tile + b, virtual, stride=virtual), :] for b in range(per_tile)], axis=0
                )
                acc[0, tile, rows, :] = mixed.T

        first = 0
        for part, many in enumerate(shares(occ_local)):
            @pl.loop(0, occupied // occ_local * many)
            def _(r, part=part, many=many, first=first):
                i = r // many * occ_local + first + r % many
                there = jnp.bitwise_xor(r // many, place[1])
                if part == 0 and occupied == 4 * occ_local:
                    there = there % 2 * 2 + there // 2
                to = pl.ds(pl.multiple_of(r % many * occupied, occupied), occupied)
                rows = pl.ds(pl.multiple_of(i * occupied, occupied), occupied)
                for far in range(tiles):
                    tile = jnp.bitwise_xor(place[2], far)
                    value = xs[tile, rows, :] + acc[0, tile, pl.ds(i, occupied, stride=occupied), :]
                    if part < 2:
                        out_refs[2 * part + far % 2][there, far // 2, to, :] = value
                    else:
                        out_refs[2 * part + far % 2][far // 2, there, to, :] = value
            first += many


def shares(occ_local):
    last = occ_local // 4
    return (occ_local - last) // 2, occ_local - last - (occ_local - last) // 2, last


def ladder(amplitudes, ladder_integrals, occ_irrep, vir_tile_irrep, first_c, occ_at, vir_at, occ_local):
    occupied, _, cd_local = amplitudes.shape
    virtual = ladder_integrals.shape[0]
    local_c = cd_local // NV
    cs = math.gcd(local_c, TILE, 8)
    assert cs % 2 == 0 and local_c * NV == cd_local and occupied == virtual and LANES % virtual == 0
    groups = NV // LANES
    steps = local_c // cs
    tiles = virtual * virtual // LANES
    place = jnp.stack([first_c, occ_at, vir_at]).astype(jnp.int32)
    ycode = jnp.broadcast_to(occ_irrep[:, None], (occupied, LANES)).astype(jnp.int32)

    def columns(c):
        return pl.BlockSpec((occupied, occupied, LANES), lambda k, g, *_: (0, 0, (k * cs + c) * groups + g))

    pieces, piece_specs = [], []
    for part, many in enumerate(shares(occ_local)):
        ahead = (occupied // occ_local, tiles // 2)
        shape = (ahead if part < 2 else ahead[::-1]) + (many * occupied, LANES)
        pieces += [jax.ShapeDtypeStruct(shape, jnp.float32)] * 2
        piece_specs += [pl.BlockSpec(shape, lambda k, g, *_: (0, 0, 0, 0))] * 2
    slots = -(-occupied // CHUNK) * CHUNK
    return pl.pallas_call(
        functools.partial(ladder_kernel, cs=cs, occ_local=occ_local, steps=steps),
        out_shape=tuple(pieces),
        grid_spec=pltpu.PrefetchScalarGridSpec(
            num_scalar_prefetch=3,
            grid=(steps, groups),
            in_specs=[pl.BlockSpec((occupied, LANES), lambda k, g, *_: (0, 0))]
            + [columns(c) for c in range(cs)] * 2,
            out_specs=tuple(piece_specs),
            scratch_shapes=[
                pltpu.VMEM((IRREPS, tiles, slots * occupied, LANES), jnp.float32),
                pltpu.VMEM((2 * CHUNK * occupied, cs * LANES), jnp.bfloat16),
                pltpu.VMEM((tiles * LANES, LANES), jnp.float32),
                pltpu.VMEM((tiles, occupied * occupied, LANES), jnp.float32),
                pltpu.VMEM((IRREPS + 1, occupied, LANES), jnp.bfloat16),
                pltpu.SMEM((slots * IRREPS,), jnp.int32),
                pltpu.SMEM((occupied,), jnp.int32),
                pltpu.SMEM((8,), jnp.int32),
            ],
        ),
        compiler_params=pltpu.CompilerParams(
            dimension_semantics=("arbitrary", "arbitrary"), vmem_limit_bytes=56 * 1024 * 1024
        ),
    )(occ_irrep, vir_tile_irrep, place, ycode, *([amplitudes] * cs), *([ladder_integrals] * cs))


def swap(values, axis, bit):
    size = lax.axis_size(axis)
    return lax.ppermute(values, axis, [(n, n ^ bit) for n in range(size)])


def owned_sum(pieces):
    arrived = [swap(pieces[2 * part + 1], "vir", 1) for part in range(3)]
    kept = [pieces[2 * part] for part in range(3)]
    order = [(1, 2), (2, 1)]
    far = [kept[part][2:] + arrived[part][2:] for part in range(2)]
    *far, held, came = lax.optimization_barrier((*far, kept[2], arrived[2]))
    first = [swap(far[part], "occ", order[part][0]) for part in range(2)]
    along = held[0] + came[0]
    for away in range(1, held.shape[0]):
        along = along + swap(held[away] + came[away], "vir", 2 * away)
    second = [
        swap(kept[part][1] + arrived[part][1] + first[part][1], "occ", order[part][1]) for part in range(2)
    ]
    mine = jnp.concatenate(
        [kept[part][0] + arrived[part][0] + first[part][0] + second[part] for part in range(2)], axis=1
    )
    total, last = mine[0], along[0]
    for away in range(1, mine.shape[0]):
        total = total + swap(mine[away], "vir", 2 * away)
    for away in range(1, along.shape[0]):
        last = last + swap(along[away], "occ", away)
    return jnp.concatenate([total, last], axis=0)


def local(amplitudes, ladder_integrals, driver, occ_energy, vir_energy, occ_irrep, vir_tile_irrep):
    occ_groups = lax.axis_size("occ")
    vir_groups = lax.axis_size("vir")
    occupied = amplitudes.shape[0]
    virtual = ladder_integrals.shape[0]
    occ_local = occupied // occ_groups
    vir_local = virtual // vir_groups
    rank = lax.axis_index(("occ", "vir"))
    occ_rank = lax.axis_index("occ")
    vir_rank = lax.axis_index("vir")
    first_c = rank * (amplitudes.shape[2] // NV)
    tiles = virtual * virtual // LANES
    direct = vir_groups == tiles == 8 and occ_groups == 4
    here = (occ_rank, vir_rank) if direct else (0 * occ_rank, 0 * vir_rank)
    pieces = ladder(amplitudes, ladder_integrals, occ_irrep, vir_tile_irrep, first_c, *here, occ_local)
    if direct:
        owned = owned_sum(pieces).reshape(occ_local, occupied, vir_local, virtual)
    else:
        parts = [jnp.stack([pieces[2 * p], pieces[2 * p + 1]], axis=2) for p in range(3)]
        if occ_groups == 4:
            parts[0] = parts[0][jnp.array([0, 2, 1, 3])]
        parts[2] = parts[2].transpose(1, 0, 2, 3, 4)
        term = jnp.concatenate(parts, axis=3).transpose(1, 2, 0, 3, 4).reshape(
            tiles, occ_groups, occ_local, occupied, vir_groups // tiles, vir_local, virtual
        )
        term = term.transpose(1, 0, 4, 2, 3, 5, 6).reshape(
            occ_groups * vir_groups, occ_local, occupied, vir_local, virtual
        )
        owned = lax.psum_scatter(term, ("occ", "vir"), scatter_dimension=0, tiled=True)[0]
    own_occ = lax.dynamic_slice_in_dim(occ_energy, occ_rank * occ_local, occ_local, 0)
    own_vir = lax.dynamic_slice_in_dim(vir_energy, vir_rank * vir_local, vir_local, 0)
    denom = (
        own_occ[:, None, None, None]
        + occ_energy[None, None, :, None]
        - own_vir[None, :, None, None]
        - vir_energy[None, None, None, :]
    )
    shaped = driver.reshape(occ_local, vir_local, occupied, virtual) + owned.transpose(0, 2, 1, 3)
    return (shaped / denom).reshape(occ_local, vir_local, occupied * virtual)


def solution(mesh):
    return jax.shard_map(
        local,
        mesh=mesh,
        in_specs=(
            P(None, None, ("occ", "vir")),
            P(None, None, ("occ", "vir")),
            P("occ", "vir", None),
            P(),
            P(),
            P(),
            P(),
        ),
        out_specs=P("occ", "vir", None),
        check_vma=False,
    )
```

```python
import functools
import math

import jax
import jax.numpy as jnp
from jax import lax
from jax.experimental import pallas as pl
from jax.experimental.pallas import tpu as pltpu
from jax.sharding import PartitionSpec as P

NV = 768
TILE = 64
LANES = 128
IRREPS = 4
SIZES = (10, 12)
CHUNK = 16


def ladder_kernel(occ_irrep, vir_irrep, place, ycode_ref, t_hbm, v_hbm, *refs, cs, occ_local, steps):
    out_refs = refs[:4]
    t_buf, v_buf, acc, tp, zs, xs, codes, table, slot_of, count, sems = refs[4:]
    occupied = t_hbm.shape[0]
    virtual = v_hbm.shape[0]
    groups = NV // LANES
    tiles = virtual * virtual // LANES
    per_tile = LANES // virtual
    lane = lax.broadcasted_iota(jnp.int32, (occupied, LANES), 1)
    band = 2 * LANES // virtual

    def copies(step, slot):
        made = []
        for c in range(cs):
            start = pl.multiple_of((step // groups * cs + c) * NV + step % groups * LANES, LANES)
            for which, (src, dst) in enumerate(((t_hbm, t_buf), (v_hbm, v_buf))):
                made.append(pltpu.make_async_copy(
                    src.at[:, :, pl.ds(start, LANES)], dst.at[slot, c], sems.at[slot, which, c]
                ))
        return made

    for copy in copies(0, 0):
        copy.start()

    for x in range(IRREPS):
        count[x] = 0

    @pl.loop(0, table.shape[0])
    def _(s):
        table[s] = 0

    @pl.loop(0, occupied)
    def _(i):
        x = occ_irrep[i]
        s = count[x]
        table[s * IRREPS + x] = i
        slot_of[i] = s
        count[x] = s + 1

    most = jnp.maximum(jnp.maximum(count[0], count[1]), jnp.maximum(count[2], count[3]))
    count[IRREPS] = most
    for label in range(IRREPS):
        codes[label] = jnp.bitwise_xor(ycode_ref[...], label).astype(jnp.float32).astype(jnp.bfloat16)
    codes[IRREPS] = (lane // (LANES // 2)).astype(jnp.float32).astype(jnp.bfloat16)

    @pl.loop(0, most)
    def _(s):
        rows = pl.ds(pl.multiple_of(s * occupied, occupied), occupied)
        for label in range(IRREPS):
            for tile in range(tiles):
                acc[label, tile, rows, :] = jnp.zeros((occupied, LANES), jnp.float32)

    most = count[IRREPS]

    first_half = codes[IRREPS] == 0

    def paired(first, second):
        turned = pltpu.roll(second, LANES // 2, second.ndim - 1)
        mask = first_half if first.ndim == 2 else jnp.broadcast_to(first_half[None], first.shape)
        return jnp.where(mask, first, turned), jnp.where(mask, turned, first)

    def work(size, base, step, slot):
        rows_all = size * occupied
        g = step % groups
        c_label = vir_irrep[(place[0] + step // groups * cs) // TILE]
        labels = [jnp.bitwise_xor(c_label, vir_irrep[2 * g + h]) for h in range(2)]
        z = jnp.where(first_half, codes[labels[0]], codes[labels[1]])
        masks = [z == x for x in range(IRREPS - 1)]
        for s in range(size):
            ids = [table[(base + s) * IRREPS + x] for x in range(IRREPS)]
            merged = []
            for c in range(cs):
                out = t_buf[slot, c, ids[IRREPS - 1]]
                for x in range(IRREPS - 1):
                    out = jnp.where(masks[x], t_buf[slot, c, ids[x]], out)
                merged.append(out)
            for p in range(cs // 2):
                halves = paired(merged[2 * p], merged[2 * p + 1])
                for h in range(2):
                    tp[h, p, s * occupied:(s + 1) * occupied, :] = halves[h]
        at = pl.ds(pl.multiple_of(base * occupied, occupied), rows_all)
        for n in range(virtual // band):
            blocks = [v_buf[slot, c, n * band:(n + 1) * band] for c in range(cs)]
            pairs = [paired(blocks[2 * p], blocks[2 * p + 1]) for p in range(cs // 2)]
            for h in range(2):
                weights = jnp.concatenate([pair[h].reshape(2 * LANES, LANES) for pair in pairs], axis=1)
                rows = jnp.concatenate([tp[h, p, :rows_all, :] for p in range(cs // 2)], axis=1)
                part = lax.dot_general(
                    rows, weights, (((1,), (1,)), ((), ())), preferred_element_type=jnp.float32
                )
                acc[labels[h], 2 * n, at, :] += part[:, :LANES]
                acc[labels[h], 2 * n + 1, at, :] += part[:, LANES:]

    @pl.loop(0, steps * groups)
    def _(step):
        slot = step % 2

        @pl.when(step + 1 < steps * groups)
        def _():
            for copy in copies(step + 1, 1 - slot):
                copy.start()

        for copy in copies(step, slot):
            copy.wait()

        low = 0
        for size in SIZES:
            @pl.when((most > low) & (most <= size))
            def _(size=size):
                work(size, 0, step, slot)
            low = size

        @pl.when(most > low)
        def _():
            @pl.loop(0, (most + CHUNK - 1) // CHUNK)
            def _(r):
                work(CHUNK, r * CHUNK, step, slot)

    @pl.loop(0, occupied)
    def _(i):
        x = occ_irrep[i]
        rows = pl.ds(pl.multiple_of(slot_of[i] * occupied, occupied), occupied)
        to = pl.ds(pl.multiple_of(i * occupied, occupied), occupied)
        hit = [ycode_ref[...] == jnp.bitwise_xor(x, label) for label in range(IRREPS - 1)]
        for tile in range(tiles):
            out = acc[IRREPS - 1, tile, rows, :]
            for label in range(IRREPS - 1):
                out = jnp.where(hit[label], acc[label, tile, rows, :], out)
            xs[tile, to, :] = out

    @pl.loop(0, occupied * occupied // LANES)
    def _(r):
        rows = pl.ds(pl.multiple_of(r * LANES, LANES), LANES)
        for tile in range(tiles):
            zs[tile * LANES:(tile + 1) * LANES, :] = xs[tile, rows, :].T
        for tile in range(tiles):
            mixed = jnp.concatenate(
                [zs[pl.ds(tile * per_tile + b, virtual, stride=virtual), :] for b in range(per_tile)], axis=0
            )
            acc[0, tile, rows, :] = mixed.T

    near = occ_local // 2
    for part in range(2):
        @pl.loop(0, occupied // occ_local * near)
        def _(r, part=part):
            i = r // near * occ_local + part * near + r % near
            there = jnp.bitwise_xor(r // near, place[1])
            if part == 0 and occupied == 4 * occ_local:
                there = there % 2 * 2 + there // 2
            to = pl.ds(pl.multiple_of(r % near * occupied, occupied), occupied)
            rows = pl.ds(pl.multiple_of(i * occupied, occupied), occupied)
            for far in range(tiles):
                tile = jnp.bitwise_xor(place[2], far)
                value = xs[tile, rows, :] + acc[0, tile, pl.ds(i, occupied, stride=occupied), :]
                out_refs[2 * part + far % 2][there, far // 2, to, :] = value


def ladder(amplitudes, ladder_integrals, occ_irrep, vir_tile_irrep, first_c, occ_at, vir_at, occ_local):
    occupied, _, cd_local = amplitudes.shape
    virtual = ladder_integrals.shape[0]
    local_c = cd_local // NV
    cs = math.gcd(local_c, TILE, 8)
    assert cs % 2 == 0 and local_c * NV == cd_local and occupied == virtual and LANES % virtual == 0
    steps = local_c // cs
    tiles = virtual * virtual // LANES
    place = jnp.stack([first_c, occ_at, vir_at]).astype(jnp.int32)
    ycode = jnp.broadcast_to(occ_irrep[:, None], (occupied, LANES)).astype(jnp.int32)

    piece = jax.ShapeDtypeStruct(
        (occupied // occ_local, tiles // 2, occ_local // 2 * occupied, LANES), jnp.float32
    )
    slots = -(-occupied // CHUNK) * CHUNK
    return pl.pallas_call(
        functools.partial(ladder_kernel, cs=cs, occ_local=occ_local, steps=steps),
        out_shape=(piece,) * 4,
        grid_spec=pltpu.PrefetchScalarGridSpec(
            num_scalar_prefetch=3,
            grid=(),
            in_specs=[pl.BlockSpec(memory_space=pltpu.VMEM)] + [pl.BlockSpec(memory_space=pl.ANY)] * 2,
            out_specs=(pl.BlockSpec(memory_space=pltpu.VMEM),) * 4,
            scratch_shapes=[
                pltpu.VMEM((2, cs, occupied, occupied, LANES), jnp.bfloat16),
                pltpu.VMEM((2, cs, virtual, virtual, LANES), jnp.bfloat16),
                pltpu.VMEM((IRREPS, tiles, slots * occupied, LANES), jnp.float32),
                pltpu.VMEM((2, cs // 2, CHUNK * occupied, LANES), jnp.bfloat16),
                pltpu.VMEM((tiles * LANES, LANES), jnp.float32),
                pltpu.VMEM((tiles, occupied * occupied, LANES), jnp.float32),
                pltpu.VMEM((IRREPS + 1, occupied, LANES), jnp.bfloat16),
                pltpu.SMEM((slots * IRREPS,), jnp.int32),
                pltpu.SMEM((occupied,), jnp.int32),
                pltpu.SMEM((8,), jnp.int32),
                pltpu.SemaphoreType.DMA((2, 2, cs)),
            ],
        ),
        compiler_params=pltpu.CompilerParams(vmem_limit_bytes=42 * 1024 * 1024),
    )(occ_irrep, vir_tile_irrep, place, ycode, amplitudes, ladder_integrals)


def swap(values, axis, bit):
    size = lax.axis_size(axis)
    return lax.ppermute(values, axis, [(n, n ^ bit) for n in range(size)])


def owned_sum(pieces):
    arrived = [swap(pieces[2 * part + 1], "vir", 1) for part in range(2)]
    order = [(1, 2), (2, 1)]
    kept = [pieces[2 * part] for part in range(2)]
    first = [swap(kept[part][2:] + arrived[part][2:], "occ", order[part][0]) for part in range(2)]
    second = [
        swap(kept[part][1] + arrived[part][1] + first[part][1], "occ", order[part][1]) for part in range(2)
    ]
    mine = jnp.stack(
        [kept[part][0] + arrived[part][0] + first[part][0] + second[part] for part in range(2)], axis=1
    )
    total = mine[0]
    for away in range(1, mine.shape[0]):
        total = total + swap(mine[away], "vir", 2 * away)
    return total


def local(amplitudes, ladder_integrals, driver, occ_energy, vir_energy, occ_irrep, vir_tile_irrep):
    occ_groups = lax.axis_size("occ")
    vir_groups = lax.axis_size("vir")
    occupied = amplitudes.shape[0]
    virtual = ladder_integrals.shape[0]
    occ_local = occupied // occ_groups
    vir_local = virtual // vir_groups
    rank = lax.axis_index(("occ", "vir"))
    occ_rank = lax.axis_index("occ")
    vir_rank = lax.axis_index("vir")
    first_c = rank * (amplitudes.shape[2] // NV)
    tiles = virtual * virtual // LANES
    direct = vir_groups == tiles == 8 and occ_groups == 4
    here = (occ_rank, vir_rank) if direct else (0 * occ_rank, 0 * vir_rank)
    pieces = ladder(amplitudes, ladder_integrals, occ_irrep, vir_tile_irrep, first_c, *here, occ_local)
    if direct:
        owned = owned_sum(pieces).reshape(occ_local, occupied, vir_local, virtual)
    else:
        halves = [jnp.stack([pieces[2 * p], pieces[2 * p + 1]], axis=2) for p in range(2)]
        if occ_groups == 4:
            halves[0] = halves[0][jnp.array([0, 2, 1, 3])]
        term = jnp.stack(halves, axis=3).transpose(1, 2, 0, 3, 4, 5).reshape(
            tiles, occ_groups, occ_local, occupied, vir_groups // tiles, vir_local, virtual
        )
        term = term.transpose(1, 0, 4, 2, 3, 5, 6).reshape(
            occ_groups * vir_groups, occ_local, occupied, vir_local, virtual
        )
        owned = lax.psum_scatter(term, ("occ", "vir"), scatter_dimension=0, tiled=True)[0]
    own_occ = lax.dynamic_slice_in_dim(occ_energy, occ_rank * occ_local, occ_local, 0)
    own_vir = lax.dynamic_slice_in_dim(vir_energy, vir_rank * vir_local, vir_local, 0)
    denom = (
        own_occ[:, None, None, None]
        + occ_energy[None, None, :, None]
        - own_vir[None, :, None, None]
        - vir_energy[None, None, None, :]
    )
    shaped = driver.reshape(occ_local, vir_local, occupied, virtual) + owned.transpose(0, 2, 1, 3)
    return (shaped / denom).reshape(occ_local, vir_local, occupied * virtual)


def solution(mesh):
    return jax.shard_map(
        local,
        mesh=mesh,
        in_specs=(
            P(None, None, ("occ", "vir")),
            P(None, None, ("occ", "vir")),
            P("occ", "vir", None),
            P(),
            P(),
            P(),
            P(),
        ),
        out_specs=P("occ", "vir", None),
        check_vma=False,
    )
```

```python
import functools
import math

import jax
import jax.numpy as jnp
from jax import lax
from jax.experimental import pallas as pl
from jax.experimental.pallas import tpu as pltpu
from jax.sharding import PartitionSpec as P

NV = 768
TILE = 64
LANES = 128
IRREPS = 4
SIZES = (10, 12)
CHUNK = 16


def ladder_kernel(occ_irrep, vir_irrep, place, ycode_ref, t_hbm, v_hbm, *refs, cs, occ_local, steps):
    out_refs = refs[:4]
    t_buf, v_buf, acc, tp_even, tp_odd, zs, xs, codes, table, slot_of, count, sems = refs[4:]
    occupied = t_hbm.shape[0]
    virtual = v_hbm.shape[0]
    groups = NV // LANES
    tiles = virtual * virtual // LANES
    per_tile = LANES // virtual
    lane = lax.broadcasted_iota(jnp.int32, (occupied, LANES), 1)
    band = 2 * LANES // virtual

    total = steps * groups

    def copies(which, step):
        src, dst = ((t_hbm, t_buf), (v_hbm, v_buf))[which]
        made = []
        for c in range(cs):
            start = pl.multiple_of((step // groups * cs + c) * NV + step % groups * LANES, LANES)
            made.append(pltpu.make_async_copy(
                src.at[:, :, pl.ds(start, LANES)], dst.at[step % 2, c], sems.at[step % 2, which, c]
            ))
        return made

    def start_all(which, step):
        for copy in copies(which, step):
            copy.start()

    def wait_all(which, step):
        for copy in copies(which, step):
            copy.wait()

    start_all(0, 0)
    start_all(1, 0)
    start_all(0, 1)

    for x in range(IRREPS):
        count[x] = 0

    @pl.loop(0, table.shape[0])
    def _(s):
        table[s] = 0

    @pl.loop(0, occupied)
    def _(i):
        x = occ_irrep[i]
        s = count[x]
        table[s * IRREPS + x] = i
        slot_of[i] = s
        count[x] = s + 1

    most = jnp.maximum(jnp.maximum(count[0], count[1]), jnp.maximum(count[2], count[3]))
    count[IRREPS] = most
    for label in range(IRREPS):
        codes[label] = jnp.bitwise_xor(ycode_ref[...], label).astype(jnp.float32).astype(jnp.bfloat16)
    codes[IRREPS] = (lane // (LANES // 2)).astype(jnp.float32).astype(jnp.bfloat16)

    @pl.loop(0, most)
    def _(s):
        rows = pl.ds(pl.multiple_of(s * occupied, occupied), occupied)
        for label in range(IRREPS):
            for tile in range(tiles):
                acc[label, tile, rows, :] = jnp.zeros((occupied, LANES), jnp.float32)

    most = count[IRREPS]

    first_half = codes[IRREPS] == 0

    def paired(first, second):
        turned = pltpu.roll(second, LANES // 2, second.ndim - 1)
        mask = first_half if first.ndim == 2 else jnp.broadcast_to(first_half[None], first.shape)
        return jnp.where(mask, first, turned), jnp.where(mask, turned, first)

    def labels_of(step):
        c_label = vir_irrep[(place[0] + step // groups * cs) // TILE]
        return [jnp.bitwise_xor(c_label, vir_irrep[2 * (step % groups) + h]) for h in range(2)]

    def build(tp, step, base, slots):
        labels = labels_of(jnp.minimum(step, total - 1))
        z = jnp.where(first_half, codes[labels[0]], codes[labels[1]])
        masks = [z == x for x in range(IRREPS - 1)]
        held = step % 2
        for s in slots:
            ids = [table[(base + s) * IRREPS + x] for x in range(IRREPS)]
            merged = []
            for c in range(cs):
                out = t_buf[held, c, ids[IRREPS - 1]]
                for x in range(IRREPS - 1):
                    out = jnp.where(masks[x], t_buf[held, c, ids[x]], out)
                merged.append(out)
            for p in range(cs // 2):
                halves = paired(merged[2 * p], merged[2 * p + 1])
                for h in range(2):
                    tp[h, p, s * occupied:(s + 1) * occupied, :] = halves[h]

    def work(size, base, step, held, tp, following):
        rows_all = size * occupied
        labels = labels_of(step)
        at = pl.ds(pl.multiple_of(base * occupied, occupied), rows_all)
        bands = virtual // band
        for n in range(bands):
            blocks = [v_buf[held, c, n * band:(n + 1) * band] for c in range(cs)]
            pairs = [paired(blocks[2 * p], blocks[2 * p + 1]) for p in range(cs // 2)]
            for h in range(2):
                weights = jnp.concatenate([pair[h].reshape(2 * LANES, LANES) for pair in pairs], axis=1)
                rows = jnp.concatenate([tp[h, p, :rows_all, :] for p in range(cs // 2)], axis=1)
                part = lax.dot_general(
                    rows, weights, (((1,), (1,)), ((), ())), preferred_element_type=jnp.float32
                )
                acc[labels[h], 2 * n, at, :] += part[:, :LANES]
                acc[labels[h], 2 * n + 1, at, :] += part[:, LANES:]
            build(following, step + 1, base, range(n * size // bands, (n + 1) * size // bands))

    def run(size, base):
        wait_all(0, 0)
        build(tp_even, 0, base, range(size))

        @pl.loop(0, total // 2)
        def _(r):
            for held, tp, following in ((0, tp_even, tp_odd), (1, tp_odd, tp_even)):
                step = 2 * r + held

                @pl.when(step + 1 < total)
                def _():
                    start_all(1, step + 1)

                @pl.when(step + 2 < total)
                def _():
                    start_all(0, step + 2)

                wait_all(1, step)

                @pl.when(step + 1 < total)
                def _():
                    wait_all(0, step + 1)

                work(size, base, step, held, tp, following)

    def begin():
        start_all(0, 0)
        start_all(1, 0)
        start_all(0, 1)

    low = 0
    for size in SIZES:
        @pl.when((most > low) & (most <= size))
        def _(size=size):
            run(size, 0)
        low = size

    @pl.when(most > low)
    def _():
        @pl.loop(0, (most + CHUNK - 1) // CHUNK)
        def _(r):
            @pl.when(r > 0)
            def _():
                begin()

            run(CHUNK, r * CHUNK)

    @pl.loop(0, occupied)
    def _(i):
        x = occ_irrep[i]
        rows = pl.ds(pl.multiple_of(slot_of[i] * occupied, occupied), occupied)
        to = pl.ds(pl.multiple_of(i * occupied, occupied), occupied)
        hit = [ycode_ref[...] == jnp.bitwise_xor(x, label) for label in range(IRREPS - 1)]
        for tile in range(tiles):
            out = acc[IRREPS - 1, tile, rows, :]
            for label in range(IRREPS - 1):
                out = jnp.where(hit[label], acc[label, tile, rows, :], out)
            xs[tile, to, :] = out

    @pl.loop(0, occupied * occupied // LANES)
    def _(r):
        rows = pl.ds(pl.multiple_of(r * LANES, LANES), LANES)
        for tile in range(tiles):
            zs[tile * LANES:(tile + 1) * LANES, :] = xs[tile, rows, :].T
        for tile in range(tiles):
            mixed = jnp.concatenate(
                [zs[pl.ds(tile * per_tile + b, virtual, stride=virtual), :] for b in range(per_tile)], axis=0
            )
            acc[0, tile, rows, :] = mixed.T

    near = occ_local // 2
    for part in range(2):
        @pl.loop(0, occupied // occ_local * near)
        def _(r, part=part):
            i = r // near * occ_local + part * near + r % near
            there = jnp.bitwise_xor(r // near, place[1])
            if part == 0 and occupied == 4 * occ_local:
                there = there % 2 * 2 + there // 2
            to = pl.ds(pl.multiple_of(r % near * occupied, occupied), occupied)
            rows = pl.ds(pl.multiple_of(i * occupied, occupied), occupied)
            for far in range(tiles):
                tile = jnp.bitwise_xor(place[2], far)
                value = xs[tile, rows, :] + acc[0, tile, pl.ds(i, occupied, stride=occupied), :]
                out_refs[2 * part + far % 2][there, far // 2, to, :] = value


def ladder(amplitudes, ladder_integrals, occ_irrep, vir_tile_irrep, first_c, occ_at, vir_at, occ_local):
    occupied, _, cd_local = amplitudes.shape
    virtual = ladder_integrals.shape[0]
    local_c = cd_local // NV
    cs = math.gcd(local_c, TILE, 8)
    assert cs % 2 == 0 and local_c * NV == cd_local and occupied == virtual and LANES % virtual == 0
    steps = local_c // cs
    assert steps * (NV // LANES) % 2 == 0
    tiles = virtual * virtual // LANES
    place = jnp.stack([first_c, occ_at, vir_at]).astype(jnp.int32)
    ycode = jnp.broadcast_to(occ_irrep[:, None], (occupied, LANES)).astype(jnp.int32)

    piece = jax.ShapeDtypeStruct(
        (occupied // occ_local, tiles // 2, occ_local // 2 * occupied, LANES), jnp.float32
    )
    slots = -(-occupied // CHUNK) * CHUNK
    return pl.pallas_call(
        functools.partial(ladder_kernel, cs=cs, occ_local=occ_local, steps=steps),
        out_shape=(piece,) * 4,
        grid_spec=pltpu.PrefetchScalarGridSpec(
            num_scalar_prefetch=3,
            grid=(),
            in_specs=[pl.BlockSpec(memory_space=pltpu.VMEM)] + [pl.BlockSpec(memory_space=pl.ANY)] * 2,
            out_specs=(pl.BlockSpec(memory_space=pltpu.VMEM),) * 4,
            scratch_shapes=[
                pltpu.VMEM((2, cs, occupied, occupied, LANES), jnp.bfloat16),
                pltpu.VMEM((2, cs, virtual, virtual, LANES), jnp.bfloat16),
                pltpu.VMEM((IRREPS, tiles, slots * occupied, LANES), jnp.float32),
                pltpu.VMEM((2, cs // 2, CHUNK * occupied, LANES), jnp.bfloat16),
                pltpu.VMEM((2, cs // 2, CHUNK * occupied, LANES), jnp.bfloat16),
                pltpu.VMEM((tiles * LANES, LANES), jnp.float32),
                pltpu.VMEM((tiles, occupied * occupied, LANES), jnp.float32),
                pltpu.VMEM((IRREPS + 1, occupied, LANES), jnp.bfloat16),
                pltpu.SMEM((slots * IRREPS,), jnp.int32),
                pltpu.SMEM((occupied,), jnp.int32),
                pltpu.SMEM((8,), jnp.int32),
                pltpu.SemaphoreType.DMA((2, 2, cs)),
            ],
        ),
        compiler_params=pltpu.CompilerParams(vmem_limit_bytes=42 * 1024 * 1024),
    )(occ_irrep, vir_tile_irrep, place, ycode, amplitudes, ladder_integrals)


def swap(values, axis, bit):
    size = lax.axis_size(axis)
    return lax.ppermute(values, axis, [(n, n ^ bit) for n in range(size)])


def owned_sum(pieces):
    arrived = [swap(pieces[2 * part + 1], "vir", 1) for part in range(2)]
    order = [(1, 2), (2, 1)]
    near, first, second = [], [], []
    for part in range(2):
        kept, came = pieces[2 * part], arrived[part]
        low, far = lax.optimization_barrier((kept[:2] + came[:2], kept[2:] + came[2:]))
        near.append(low)
        first.append(swap(far, "occ", order[part][0]))
    for part in range(2):
        low, far = lax.optimization_barrier((near[part][0] + first[part][0], near[part][1] + first[part][1]))
        near[part] = low
        second.append(swap(far, "occ", order[part][1]))
    mine = jnp.stack([near[part] + second[part] for part in range(2)], axis=1)
    total = mine[0]
    for away in range(1, mine.shape[0]):
        total = total + swap(mine[away], "vir", 2 * away)
    return total


def local(amplitudes, ladder_integrals, driver, occ_energy, vir_energy, occ_irrep, vir_tile_irrep):
    occ_groups = lax.axis_size("occ")
    vir_groups = lax.axis_size("vir")
    occupied = amplitudes.shape[0]
    virtual = ladder_integrals.shape[0]
    occ_local = occupied // occ_groups
    vir_local = virtual // vir_groups
    rank = lax.axis_index(("occ", "vir"))
    occ_rank = lax.axis_index("occ")
    vir_rank = lax.axis_index("vir")
    first_c = rank * (amplitudes.shape[2] // NV)
    tiles = virtual * virtual // LANES
    direct = vir_groups == tiles == 8 and occ_groups == 4
    here = (occ_rank, vir_rank) if direct else (0 * occ_rank, 0 * vir_rank)
    pieces = ladder(amplitudes, ladder_integrals, occ_irrep, vir_tile_irrep, first_c, *here, occ_local)
    if direct:
        owned = owned_sum(pieces).reshape(occ_local, occupied, vir_local, virtual)
    else:
        halves = [jnp.stack([pieces[2 * p], pieces[2 * p + 1]], axis=2) for p in range(2)]
        if occ_groups == 4:
            halves[0] = halves[0][jnp.array([0, 2, 1, 3])]
        term = jnp.stack(halves, axis=3).transpose(1, 2, 0, 3, 4, 5).reshape(
            tiles, occ_groups, occ_local, occupied, vir_groups // tiles, vir_local, virtual
        )
        term = term.transpose(1, 0, 4, 2, 3, 5, 6).reshape(
            occ_groups * vir_groups, occ_local, occupied, vir_local, virtual
        )
        owned = lax.psum_scatter(term, ("occ", "vir"), scatter_dimension=0, tiled=True)[0]
    own_occ = lax.dynamic_slice_in_dim(occ_energy, occ_rank * occ_local, occ_local, 0)
    own_vir = lax.dynamic_slice_in_dim(vir_energy, vir_rank * vir_local, vir_local, 0)
    denom = (
        own_occ[:, None, None, None]
        + occ_energy[None, None, :, None]
        - own_vir[None, :, None, None]
        - vir_energy[None, None, None, :]
    )
    shaped = driver.reshape(occ_local, vir_local, occupied, virtual) + owned.transpose(0, 2, 1, 3)
    return (shaped / denom).reshape(occ_local, vir_local, occupied * virtual)


def solution(mesh):
    return jax.shard_map(
        local,
        mesh=mesh,
        in_specs=(
            P(None, None, ("occ", "vir")),
            P(None, None, ("occ", "vir")),
            P("occ", "vir", None),
            P(),
            P(),
            P(),
            P(),
        ),
        out_specs=P("occ", "vir", None),
        check_vma=False,
    )
```

```python
import functools
import math

import jax
import jax.numpy as jnp
from jax import lax
from jax.experimental import pallas as pl
from jax.experimental.pallas import tpu as pltpu
from jax.sharding import PartitionSpec as P

NV = 768
TILE = 64
LANES = 128
IRREPS = 4
SIZES = (10, 12)
CHUNK = 16


def ladder_kernel(facts, ycode_ref, t_hbm, v_hbm, *refs, cs, occ_local, steps):
    out_refs = refs[:4]
    t_buf, v_buf, acc, tp_even, tp_odd, zs, xs, codes, table, slot_of, count, sems = refs[4:]
    occupied = t_hbm.shape[0]
    place, occ_irrep, vir_irrep = (facts.at[pl.ds(n, many)] for n, many in ((0, 8), (8, occupied), (8 + occupied, NV // TILE)))
    virtual = v_hbm.shape[0]
    groups = NV // LANES
    tiles = virtual * virtual // LANES
    per_tile = LANES // virtual
    lane = lax.broadcasted_iota(jnp.int32, (occupied, LANES), 1)
    band = 2 * LANES // virtual

    total = steps * groups

    def copies(which, step):
        src, dst = ((t_hbm, t_buf), (v_hbm, v_buf))[which]
        made = []
        for c in range(cs):
            start = pl.multiple_of((step // groups * cs + c) * NV + step % groups * LANES, LANES)
            made.append(pltpu.make_async_copy(
                src.at[:, :, pl.ds(start, LANES)], dst.at[step % 2, c], sems.at[step % 2, which, c]
            ))
        return made

    def start_all(which, step):
        for copy in copies(which, step):
            copy.start()

    def wait_all(which, step):
        for copy in copies(which, step):
            copy.wait()

    start_all(0, 0)
    start_all(1, 0)
    start_all(0, 1)

    for x in range(IRREPS):
        count[x] = 0

    @pl.loop(0, table.shape[0])
    def _(s):
        table[s] = 0

    @pl.loop(0, occupied)
    def _(i):
        x = occ_irrep[i]
        s = count[x]
        table[s * IRREPS + x] = i
        slot_of[i] = s
        count[x] = s + 1

    most = jnp.maximum(jnp.maximum(count[0], count[1]), jnp.maximum(count[2], count[3]))
    count[IRREPS] = most
    for label in range(IRREPS):
        codes[label] = jnp.bitwise_xor(ycode_ref[...], label).astype(jnp.float32).astype(jnp.bfloat16)
    codes[IRREPS] = (lane // (LANES // 2)).astype(jnp.float32).astype(jnp.bfloat16)

    @pl.loop(0, most)
    def _(s):
        rows = pl.ds(pl.multiple_of(s * occupied, occupied), occupied)
        for label in range(IRREPS):
            for tile in range(tiles):
                acc[label, tile, rows, :] = jnp.zeros((occupied, LANES), jnp.float32)

    most = count[IRREPS]

    first_half = codes[IRREPS] == 0
    first_turned = pltpu.roll(codes[IRREPS], LANES // 2, 1) == 1

    def paired(first, second):
        turned = pltpu.roll(second, LANES // 2, second.ndim - 1)
        mask = first_half if first.ndim == 2 else jnp.broadcast_to(first_turned[None], first.shape)
        return jnp.where(mask, first, turned), jnp.where(mask, turned, first)

    def labels_of(step):
        c_label = vir_irrep[(place[0] + step // groups * cs) // TILE]
        return [jnp.bitwise_xor(c_label, vir_irrep[2 * (step % groups) + h]) for h in range(2)]

    def build(tp, step, base, slots):
        labels = labels_of(jnp.minimum(step, total - 1))
        z = jnp.where(first_half, codes[labels[0]], codes[labels[1]])
        masks = [z == x for x in range(IRREPS - 1)]
        held = step % 2
        for s in slots:
            ids = [table[(base + s) * IRREPS + x] for x in range(IRREPS)]
            merged = []
            for c in range(cs):
                out = t_buf[held, c, ids[IRREPS - 1]]
                for x in range(IRREPS - 1):
                    out = jnp.where(masks[x], t_buf[held, c, ids[x]], out)
                merged.append(out)
            for p in range(cs // 2):
                halves = paired(merged[2 * p], merged[2 * p + 1])
                for h in range(2):
                    tp[h, p, s * occupied:(s + 1) * occupied, :] = halves[h]

    def work(size, base, step, held, tp, following):
        rows_all = size * occupied
        labels = labels_of(step)
        at = pl.ds(pl.multiple_of(base * occupied, occupied), rows_all)
        bands = virtual // band
        for n in range(bands):
            blocks = [v_buf[held, c, n * band:(n + 1) * band] for c in range(cs)]
            pairs = [paired(blocks[2 * p], blocks[2 * p + 1]) for p in range(cs // 2)]
            for h in range(2):
                weights = jnp.concatenate([pair[h].reshape(2 * LANES, LANES) for pair in pairs], axis=1)
                rows = jnp.concatenate([tp[h, p, :rows_all, :] for p in range(cs // 2)], axis=1)
                part = lax.dot_general(
                    rows, weights, (((1,), (1,)), ((), ())), preferred_element_type=jnp.float32
                )
                acc[labels[h], 2 * n, at, :] += part[:, :LANES]
                acc[labels[h], 2 * n + 1, at, :] += part[:, LANES:]
            build(following, step + 1, base, range(n * size // bands, (n + 1) * size // bands))

    def run(size, base):
        wait_all(0, 0)
        build(tp_even, 0, base, range(size))

        @pl.loop(0, total // 2)
        def _(r):
            for held, tp, following in ((0, tp_even, tp_odd), (1, tp_odd, tp_even)):
                step = 2 * r + held

                @pl.when(step + 1 < total)
                def _():
                    start_all(1, step + 1)

                @pl.when(step + 2 < total)
                def _():
                    start_all(0, step + 2)

                wait_all(1, step)

                @pl.when(step + 1 < total)
                def _():
                    wait_all(0, step + 1)

                work(size, base, step, held, tp, following)

    def begin():
        start_all(0, 0)
        start_all(1, 0)
        start_all(0, 1)

    low = 0
    for size in SIZES:
        @pl.when((most > low) & (most <= size))
        def _(size=size):
            run(size, 0)
        low = size

    @pl.when(most > low)
    def _():
        @pl.loop(0, (most + CHUNK - 1) // CHUNK)
        def _(r):
            @pl.when(r > 0)
            def _():
                begin()

            run(CHUNK, r * CHUNK)

    @pl.loop(0, occupied)
    def _(i):
        x = occ_irrep[i]
        rows = pl.ds(pl.multiple_of(slot_of[i] * occupied, occupied), occupied)
        to = pl.ds(pl.multiple_of(i * occupied, occupied), occupied)
        hit = [ycode_ref[...] == jnp.bitwise_xor(x, label) for label in range(IRREPS - 1)]
        for tile in range(tiles):
            out = acc[IRREPS - 1, tile, rows, :]
            for label in range(IRREPS - 1):
                out = jnp.where(hit[label], acc[label, tile, rows, :], out)
            xs[tile, to, :] = out

    @pl.loop(0, occupied * occupied // LANES)
    def _(r):
        rows = pl.ds(pl.multiple_of(r * LANES, LANES), LANES)
        for tile in range(tiles):
            zs[tile * LANES:(tile + 1) * LANES, :] = xs[tile, rows, :].T
        for tile in range(tiles):
            mixed = jnp.concatenate(
                [zs[pl.ds(tile * per_tile + b, virtual, stride=virtual), :] for b in range(per_tile)], axis=0
            )
            acc[0, tile, rows, :] = mixed.T

    near = occ_local // 2
    for part in range(2):
        @pl.loop(0, occupied // occ_local * near)
        def _(r, part=part):
            i = r // near * occ_local + part * near + r % near
            there = jnp.bitwise_xor(r // near, place[1])
            if part == 0 and occupied == 4 * occ_local:
                there = there % 2 * 2 + there // 2
            to = pl.ds(pl.multiple_of(r % near * occupied, occupied), occupied)
            rows = pl.ds(pl.multiple_of(i * occupied, occupied), occupied)
            for far in range(tiles):
                tile = jnp.bitwise_xor(place[2], far)
                value = xs[tile, rows, :] + acc[0, tile, pl.ds(i, occupied, stride=occupied), :]
                out_refs[2 * part + far % 2][there, far // 2, to, :] = value


def ladder(amplitudes, ladder_integrals, occ_irrep, vir_tile_irrep, first_c, occ_at, vir_at, occ_local):
    occupied, _, cd_local = amplitudes.shape
    virtual = ladder_integrals.shape[0]
    local_c = cd_local // NV
    cs = math.gcd(local_c, TILE, 8)
    assert cs % 2 == 0 and local_c * NV == cd_local and occupied == virtual and LANES % virtual == 0
    steps = local_c // cs
    assert steps * (NV // LANES) % 2 == 0
    tiles = virtual * virtual // LANES
    place = jnp.stack([first_c, occ_at, vir_at] + [0 * occ_at] * 5)
    facts = jnp.concatenate([place, occ_irrep, vir_tile_irrep]).astype(jnp.int32)
    ycode = jnp.broadcast_to(occ_irrep[:, None], (occupied, LANES)).astype(jnp.int32)

    piece = jax.ShapeDtypeStruct(
        (occupied // occ_local, tiles // 2, occ_local // 2 * occupied, LANES), jnp.float32
    )
    slots = -(-occupied // CHUNK) * CHUNK
    return pl.pallas_call(
        functools.partial(ladder_kernel, cs=cs, occ_local=occ_local, steps=steps),
        out_shape=(piece,) * 4,
        grid_spec=pltpu.PrefetchScalarGridSpec(
            num_scalar_prefetch=1,
            grid=(),
            in_specs=[pl.BlockSpec(memory_space=pltpu.VMEM)] + [pl.BlockSpec(memory_space=pl.ANY)] * 2,
            out_specs=(pl.BlockSpec(memory_space=pltpu.VMEM),) * 4,
            scratch_shapes=[
                pltpu.VMEM((2, cs, occupied, occupied, LANES), jnp.bfloat16),
                pltpu.VMEM((2, cs, virtual, virtual, LANES), jnp.bfloat16),
                pltpu.VMEM((IRREPS, tiles, slots * occupied, LANES), jnp.float32),
                pltpu.VMEM((2, cs // 2, CHUNK * occupied, LANES), jnp.bfloat16),
                pltpu.VMEM((2, cs // 2, CHUNK * occupied, LANES), jnp.bfloat16),
                pltpu.VMEM((tiles * LANES, LANES), jnp.float32),
                pltpu.VMEM((tiles, occupied * occupied, LANES), jnp.float32),
                pltpu.VMEM((IRREPS + 1, occupied, LANES), jnp.bfloat16),
                pltpu.SMEM((slots * IRREPS,), jnp.int32),
                pltpu.SMEM((occupied,), jnp.int32),
                pltpu.SMEM((8,), jnp.int32),
                pltpu.SemaphoreType.DMA((2, 2, cs)),
            ],
        ),
        compiler_params=pltpu.CompilerParams(vmem_limit_bytes=42 * 1024 * 1024),
    )(facts, ycode, amplitudes, ladder_integrals)


def swap(values, axis, bit):
    size = lax.axis_size(axis)
    return lax.ppermute(values, axis, [(n, n ^ bit) for n in range(size)])


def owned_sum(pieces):
    arrived = [swap(pieces[2 * part + 1], "vir", 1) for part in range(2)]
    order = [(1, 2), (2, 1)]
    near, first, second = [], [], []
    for part in range(2):
        kept, came = pieces[2 * part], arrived[part]
        low, far = lax.optimization_barrier((kept[:2] + came[:2], kept[2:] + came[2:]))
        near.append(low)
        first.append(swap(far, "occ", order[part][0]))
    for part in range(2):
        low, far = lax.optimization_barrier((near[part][0] + first[part][0], near[part][1] + first[part][1]))
        near[part] = low
        second.append(swap(far, "occ", order[part][1]))
    mine = jnp.stack([near[part] + second[part] for part in range(2)], axis=1)
    total = mine[0]
    for away in range(1, mine.shape[0]):
        total = total + swap(mine[away], "vir", 2 * away)
    return total


def local(amplitudes, ladder_integrals, driver, occ_energy, vir_energy, occ_irrep, vir_tile_irrep):
    occ_groups = lax.axis_size("occ")
    vir_groups = lax.axis_size("vir")
    occupied = amplitudes.shape[0]
    virtual = ladder_integrals.shape[0]
    occ_local = occupied // occ_groups
    vir_local = virtual // vir_groups
    rank = lax.axis_index(("occ", "vir"))
    occ_rank = lax.axis_index("occ")
    vir_rank = lax.axis_index("vir")
    first_c = rank * (amplitudes.shape[2] // NV)
    tiles = virtual * virtual // LANES
    direct = vir_groups == tiles == 8 and occ_groups == 4
    here = (occ_rank, vir_rank) if direct else (0 * occ_rank, 0 * vir_rank)
    pieces = ladder(amplitudes, ladder_integrals, occ_irrep, vir_tile_irrep, first_c, *here, occ_local)
    if direct:
        owned = owned_sum(pieces).reshape(occ_local, occupied, vir_local, virtual)
    else:
        halves = [jnp.stack([pieces[2 * p], pieces[2 * p + 1]], axis=2) for p in range(2)]
        if occ_groups == 4:
            halves[0] = halves[0][jnp.array([0, 2, 1, 3])]
        term = jnp.stack(halves, axis=3).transpose(1, 2, 0, 3, 4, 5).reshape(
            tiles, occ_groups, occ_local, occupied, vir_groups // tiles, vir_local, virtual
        )
        term = term.transpose(1, 0, 4, 2, 3, 5, 6).reshape(
            occ_groups * vir_groups, occ_local, occupied, vir_local, virtual
        )
        owned = lax.psum_scatter(term, ("occ", "vir"), scatter_dimension=0, tiled=True)[0]
    own_occ = lax.dynamic_slice_in_dim(occ_energy, occ_rank * occ_local, occ_local, 0)
    own_vir = lax.dynamic_slice_in_dim(vir_energy, vir_rank * vir_local, vir_local, 0)
    denom = (
        own_occ[:, None, None, None]
        + occ_energy[None, None, :, None]
        - own_vir[None, :, None, None]
        - vir_energy[None, None, None, :]
    )
    shaped = driver.reshape(occ_local, vir_local, occupied, virtual) + owned.transpose(0, 2, 1, 3)
    return (shaped / denom).reshape(occ_local, vir_local, occupied * virtual)


def solution(mesh):
    return jax.shard_map(
        local,
        mesh=mesh,
        in_specs=(
            P(None, None, ("occ", "vir")),
            P(None, None, ("occ", "vir")),
            P("occ", "vir", None),
            P(),
            P(),
            P(),
            P(),
        ),
        out_specs=P("occ", "vir", None),
        check_vma=False,
    )
```

```python
import functools
import math

import jax
import jax.numpy as jnp
from jax import lax
from jax.experimental import pallas as pl
from jax.experimental.pallas import tpu as pltpu
from jax.sharding import PartitionSpec as P

NV = 768
TILE = 64
LANES = 128
IRREPS = 4
SIZES = (10, 12)
CHUNK = 16


def ladder_kernel(facts, ycode_ref, t_hbm, v_hbm, *refs, cs, occ_local, steps):
    out_refs = refs[:4]
    t_buf, v_buf, acc, tp_even, tp_odd, zs, xs, codes, table, slot_of, count, sems = refs[4:]
    occupied = t_hbm.shape[0]
    place, occ_irrep, vir_irrep = (facts.at[pl.ds(n, many)] for n, many in ((0, 8), (8, occupied), (8 + occupied, NV // TILE)))
    virtual = v_hbm.shape[0]
    groups = NV // LANES
    tiles = virtual * virtual // LANES
    per_tile = LANES // virtual
    lane = lax.broadcasted_iota(jnp.int32, (occupied, LANES), 1)
    band = 2 * LANES // virtual

    per_block = 2
    wide = per_block * LANES
    blocks_c = groups // per_block
    total = steps * blocks_c

    def copies(which, block):
        src, dst = ((t_hbm, t_buf), (v_hbm, v_buf))[which]
        made = []
        for c in range(cs):
            start = pl.multiple_of((block // blocks_c * cs + c) * NV + block % blocks_c * wide, LANES)
            made.append(pltpu.make_async_copy(
                src.at[:, :, pl.ds(start, wide)], dst.at[block % 2, c], sems.at[block % 2, which, c]
            ))
        return made

    def start_all(which, step):
        for copy in copies(which, step):
            copy.start()

    def wait_all(which, step):
        for copy in copies(which, step):
            copy.wait()

    start_all(0, 0)
    start_all(1, 0)
    start_all(0, 1)

    for x in range(IRREPS):
        count[x] = 0

    @pl.loop(0, table.shape[0])
    def _(s):
        table[s] = 0

    @pl.loop(0, occupied)
    def _(i):
        x = occ_irrep[i]
        s = count[x]
        table[s * IRREPS + x] = i
        slot_of[i] = s
        count[x] = s + 1

    most = jnp.maximum(jnp.maximum(count[0], count[1]), jnp.maximum(count[2], count[3]))
    count[IRREPS] = most
    for label in range(IRREPS):
        codes[label] = jnp.bitwise_xor(ycode_ref[...], label).astype(jnp.float32).astype(jnp.bfloat16)
    codes[IRREPS] = (lane // (LANES // 2)).astype(jnp.float32).astype(jnp.bfloat16)

    @pl.loop(0, most)
    def _(s):
        rows = pl.ds(pl.multiple_of(s * occupied, occupied), occupied)
        for label in range(IRREPS):
            for tile in range(tiles):
                acc[label, tile, rows, :] = jnp.zeros((occupied, LANES), jnp.float32)

    most = count[IRREPS]

    first_half = codes[IRREPS] == 0
    first_turned = pltpu.roll(codes[IRREPS], LANES // 2, 1) == 1

    def paired(first, second):
        turned = pltpu.roll(second, LANES // 2, second.ndim - 1)
        mask = first_half if first.ndim == 2 else jnp.broadcast_to(first_turned[None], first.shape)
        return jnp.where(mask, first, turned), jnp.where(mask, turned, first)

    def labels_of(block, m):
        c_label = vir_irrep[(place[0] + block // blocks_c * cs) // TILE]
        first = 2 * (block % blocks_c * per_block + m)
        return [jnp.bitwise_xor(c_label, vir_irrep[first + h]) for h in range(2)]

    def build(tp, block, m, base, slots):
        labels = labels_of(jnp.minimum(block, total - 1), m)
        lanes = slice(m * LANES, (m + 1) * LANES)
        z = jnp.where(first_half, codes[labels[0]], codes[labels[1]])
        masks = [z == x for x in range(IRREPS - 1)]
        held = block % 2
        for s in slots:
            ids = [table[(base + s) * IRREPS + x] for x in range(IRREPS)]
            merged = []
            for c in range(cs):
                out = t_buf[held, c, ids[IRREPS - 1], :, lanes]
                for x in range(IRREPS - 1):
                    out = jnp.where(masks[x], t_buf[held, c, ids[x], :, lanes], out)
                merged.append(out)
            for p in range(cs // 2):
                halves = paired(merged[2 * p], merged[2 * p + 1])
                for h in range(2):
                    tp[h, p, s * occupied:(s + 1) * occupied, :] = halves[h]

    def work(size, base, block, m, tp, following):
        rows_all = size * occupied
        labels = labels_of(block, m)
        held = block % 2
        lanes = slice(m * LANES, (m + 1) * LANES)
        at = pl.ds(pl.multiple_of(base * occupied, occupied), rows_all)
        bands = virtual // band
        for n in range(bands):
            blocks = [v_buf[held, c, n * band:(n + 1) * band, :, lanes] for c in range(cs)]
            pairs = [paired(blocks[2 * p], blocks[2 * p + 1]) for p in range(cs // 2)]
            for h in range(2):
                weights = jnp.concatenate([pair[h].reshape(2 * LANES, LANES) for pair in pairs], axis=1)
                rows = jnp.concatenate([tp[h, p, :rows_all, :] for p in range(cs // 2)], axis=1)
                part = lax.dot_general(
                    rows, weights, (((1,), (1,)), ((), ())), preferred_element_type=jnp.float32
                )
                acc[labels[h], 2 * n, at, :] += part[:, :LANES]
                acc[labels[h], 2 * n + 1, at, :] += part[:, LANES:]
            build(following, block + m, 1 - m, base, range(n * size // bands, (n + 1) * size // bands))

    def run(size, base):
        wait_all(0, 0)
        build(tp_even, 0, 0, base, range(size))

        @pl.loop(0, total)
        def _(block):
            @pl.when(block + 1 < total)
            def _():
                start_all(1, block + 1)

            wait_all(1, block)
            work(size, base, block, 0, tp_even, tp_odd)

            @pl.when(block + 2 < total)
            def _():
                start_all(0, block + 2)

            @pl.when(block + 1 < total)
            def _():
                wait_all(0, block + 1)

            work(size, base, block, 1, tp_odd, tp_even)

    def begin():
        start_all(0, 0)
        start_all(1, 0)
        start_all(0, 1)

    low = 0
    for size in SIZES:
        @pl.when((most > low) & (most <= size))
        def _(size=size):
            run(size, 0)
        low = size

    @pl.when(most > low)
    def _():
        @pl.loop(0, (most + CHUNK - 1) // CHUNK)
        def _(r):
            @pl.when(r > 0)
            def _():
                begin()

            run(CHUNK, r * CHUNK)

    @pl.loop(0, occupied)
    def _(i):
        x = occ_irrep[i]
        rows = pl.ds(pl.multiple_of(slot_of[i] * occupied, occupied), occupied)
        to = pl.ds(pl.multiple_of(i * occupied, occupied), occupied)
        hit = [ycode_ref[...] == jnp.bitwise_xor(x, label) for label in range(IRREPS - 1)]
        for tile in range(tiles):
            out = acc[IRREPS - 1, tile, rows, :]
            for label in range(IRREPS - 1):
                out = jnp.where(hit[label], acc[label, tile, rows, :], out)
            xs[tile, to, :] = out

    @pl.loop(0, occupied * occupied // LANES)
    def _(r):
        rows = pl.ds(pl.multiple_of(r * LANES, LANES), LANES)
        for tile in range(tiles):
            zs[tile * LANES:(tile + 1) * LANES, :] = xs[tile, rows, :].T
        for tile in range(tiles):
            mixed = jnp.concatenate(
                [zs[pl.ds(tile * per_tile + b, virtual, stride=virtual), :] for b in range(per_tile)], axis=0
            )
            acc[0, tile, rows, :] = mixed.T

    near = occ_local // 2
    for part in range(2):
        @pl.loop(0, occupied // occ_local * near)
        def _(r, part=part):
            i = r // near * occ_local + part * near + r % near
            there = jnp.bitwise_xor(r // near, place[1])
            if part == 0 and occupied == 4 * occ_local:
                there = there % 2 * 2 + there // 2
            to = pl.ds(pl.multiple_of(r % near * occupied, occupied), occupied)
            rows = pl.ds(pl.multiple_of(i * occupied, occupied), occupied)
            for far in range(tiles):
                tile = jnp.bitwise_xor(place[2], far)
                value = xs[tile, rows, :] + acc[0, tile, pl.ds(i, occupied, stride=occupied), :]
                out_refs[2 * part + far % 2][there, far // 2, to, :] = value


def ladder(amplitudes, ladder_integrals, occ_irrep, vir_tile_irrep, first_c, occ_at, vir_at, occ_local):
    occupied, _, cd_local = amplitudes.shape
    virtual = ladder_integrals.shape[0]
    local_c = cd_local // NV
    cs = math.gcd(local_c, TILE, 8)
    assert cs % 2 == 0 and local_c * NV == cd_local and occupied == virtual and LANES % virtual == 0
    steps = local_c // cs
    assert steps * (NV // LANES) >= 4
    tiles = virtual * virtual // LANES
    place = jnp.stack([first_c, occ_at, vir_at] + [0 * occ_at] * 5)
    facts = jnp.concatenate([place, occ_irrep, vir_tile_irrep]).astype(jnp.int32)
    ycode = jnp.broadcast_to(occ_irrep[:, None], (occupied, LANES)).astype(jnp.int32)

    piece = jax.ShapeDtypeStruct(
        (occupied // occ_local, tiles // 2, occ_local // 2 * occupied, LANES), jnp.float32
    )
    slots = -(-occupied // CHUNK) * CHUNK
    return pl.pallas_call(
        functools.partial(ladder_kernel, cs=cs, occ_local=occ_local, steps=steps),
        out_shape=(piece,) * 4,
        grid_spec=pltpu.PrefetchScalarGridSpec(
            num_scalar_prefetch=1,
            grid=(),
            in_specs=[pl.BlockSpec(memory_space=pltpu.VMEM)] + [pl.BlockSpec(memory_space=pl.ANY)] * 2,
            out_specs=(pl.BlockSpec(memory_space=pltpu.VMEM),) * 4,
            scratch_shapes=[
                pltpu.VMEM((2, cs, occupied, occupied, 2 * LANES), jnp.bfloat16),
                pltpu.VMEM((2, cs, virtual, virtual, 2 * LANES), jnp.bfloat16),
                pltpu.VMEM((IRREPS, tiles, slots * occupied, LANES), jnp.float32),
                pltpu.VMEM((2, cs // 2, CHUNK * occupied, LANES), jnp.bfloat16),
                pltpu.VMEM((2, cs // 2, CHUNK * occupied, LANES), jnp.bfloat16),
                pltpu.VMEM((tiles * LANES, LANES), jnp.float32),
                pltpu.VMEM((tiles, occupied * occupied, LANES), jnp.float32),
                pltpu.VMEM((IRREPS + 1, occupied, LANES), jnp.bfloat16),
                pltpu.SMEM((slots * IRREPS,), jnp.int32),
                pltpu.SMEM((occupied,), jnp.int32),
                pltpu.SMEM((8,), jnp.int32),
                pltpu.SemaphoreType.DMA((2, 2, cs)),
            ],
        ),
        compiler_params=pltpu.CompilerParams(vmem_limit_bytes=49 * 1024 * 1024),
    )(facts, ycode, amplitudes, ladder_integrals)


def swap(values, axis, bit):
    size = lax.axis_size(axis)
    return lax.ppermute(values, axis, [(n, n ^ bit) for n in range(size)])


def owned_sum(pieces):
    arrived = [swap(pieces[2 * part + 1], "vir", 1) for part in range(2)]
    order = [(1, 2), (2, 1)]
    near, first, second = [], [], []
    for part in range(2):
        kept, came = pieces[2 * part], arrived[part]
        low, far = lax.optimization_barrier((kept[:2] + came[:2], kept[2:] + came[2:]))
        near.append(low)
        first.append(swap(far, "occ", order[part][0]))
    for part in range(2):
        low, far = lax.optimization_barrier((near[part][0] + first[part][0], near[part][1] + first[part][1]))
        near[part] = low
        second.append(swap(far, "occ", order[part][1]))
    mine = jnp.stack([near[part] + second[part] for part in range(2)], axis=1)
    total = mine[0]
    for away in range(1, mine.shape[0]):
        total = total + swap(mine[away], "vir", 2 * away)
    return total


def local(amplitudes, ladder_integrals, driver, occ_energy, vir_energy, occ_irrep, vir_tile_irrep):
    occ_groups = lax.axis_size("occ")
    vir_groups = lax.axis_size("vir")
    occupied = amplitudes.shape[0]
    virtual = ladder_integrals.shape[0]
    occ_local = occupied // occ_groups
    vir_local = virtual // vir_groups
    rank = lax.axis_index(("occ", "vir"))
    occ_rank = lax.axis_index("occ")
    vir_rank = lax.axis_index("vir")
    first_c = rank * (amplitudes.shape[2] // NV)
    tiles = virtual * virtual // LANES
    direct = vir_groups == tiles == 8 and occ_groups == 4
    here = (occ_rank, vir_rank) if direct else (0 * occ_rank, 0 * vir_rank)
    pieces = ladder(amplitudes, ladder_integrals, occ_irrep, vir_tile_irrep, first_c, *here, occ_local)
    if direct:
        owned = owned_sum(pieces).reshape(occ_local, occupied, vir_local, virtual)
    else:
        halves = [jnp.stack([pieces[2 * p], pieces[2 * p + 1]], axis=2) for p in range(2)]
        if occ_groups == 4:
            halves[0] = halves[0][jnp.array([0, 2, 1, 3])]
        term = jnp.stack(halves, axis=3).transpose(1, 2, 0, 3, 4, 5).reshape(
            tiles, occ_groups, occ_local, occupied, vir_groups // tiles, vir_local, virtual
        )
        term = term.transpose(1, 0, 4, 2, 3, 5, 6).reshape(
            occ_groups * vir_groups, occ_local, occupied, vir_local, virtual
        )
        owned = lax.psum_scatter(term, ("occ", "vir"), scatter_dimension=0, tiled=True)[0]
    own_occ = lax.dynamic_slice_in_dim(occ_energy, occ_rank * occ_local, occ_local, 0)
    own_vir = lax.dynamic_slice_in_dim(vir_energy, vir_rank * vir_local, vir_local, 0)
    denom = (
        own_occ[:, None, None, None]
        + occ_energy[None, None, :, None]
        - own_vir[None, :, None, None]
        - vir_energy[None, None, None, :]
    )
    shaped = driver.reshape(occ_local, vir_local, occupied, virtual) + owned.transpose(0, 2, 1, 3)
    return (shaped / denom).reshape(occ_local, vir_local, occupied * virtual)


def solution(mesh):
    return jax.shard_map(
        local,
        mesh=mesh,
        in_specs=(
            P(None, None, ("occ", "vir")),
            P(None, None, ("occ", "vir")),
            P("occ", "vir", None),
            P(),
            P(),
            P(),
            P(),
        ),
        out_specs=P("occ", "vir", None),
        check_vma=False,
    )
```

```python
import functools
import math

import jax
import jax.numpy as jnp
from jax import lax
from jax.experimental import pallas as pl
from jax.experimental.pallas import tpu as pltpu
from jax.sharding import PartitionSpec as P

NV = 768
TILE = 64
LANES = 128
STEPS = 3
IRREPS = 4
SIZES = (10, 12)
CHUNK = 16


def ladder_kernel(facts, ycode_ref, t_hbm, v_hbm, *refs, cs, occ_local, steps):
    out_refs = refs[:4]
    t_buf, v_buf, acc, *tps, zs, xs, codes, table, slot_of, count, sems = refs[4:]
    occupied = t_hbm.shape[0]
    place, occ_irrep, vir_irrep = (facts.at[pl.ds(n, many)] for n, many in ((0, 8), (8, occupied), (8 + occupied, NV // TILE)))
    virtual = v_hbm.shape[0]
    groups = NV // LANES
    tiles = virtual * virtual // LANES
    per_tile = LANES // virtual
    lane = lax.broadcasted_iota(jnp.int32, (occupied, LANES), 1)
    band = 2 * LANES // virtual

    per_block = len(tps)
    wide = per_block * LANES
    blocks_c = groups // per_block
    total = steps * blocks_c

    def copies(which, block):
        src, dst = ((t_hbm, t_buf), (v_hbm, v_buf))[which]
        made = []
        for c in range(cs):
            start = pl.multiple_of((block // blocks_c * cs + c) * NV + block % blocks_c * wide, LANES)
            made.append(pltpu.make_async_copy(
                src.at[:, :, pl.ds(start, wide)], dst.at[block % 2, c], sems.at[block % 2, which, c]
            ))
        return made

    def start_all(which, step):
        for copy in copies(which, step):
            copy.start()

    def wait_all(which, step):
        for copy in copies(which, step):
            copy.wait()

    start_all(0, 0)
    start_all(1, 0)
    start_all(0, 1)

    for x in range(IRREPS):
        count[x] = 0

    @pl.loop(0, table.shape[0])
    def _(s):
        table[s] = 0

    @pl.loop(0, occupied)
    def _(i):
        x = occ_irrep[i]
        s = count[x]
        table[s * IRREPS + x] = i
        slot_of[i] = s
        count[x] = s + 1

    most = jnp.maximum(jnp.maximum(count[0], count[1]), jnp.maximum(count[2], count[3]))
    count[IRREPS] = most
    for label in range(IRREPS):
        codes[label] = jnp.bitwise_xor(ycode_ref[...], label).astype(jnp.float32).astype(jnp.bfloat16)
    codes[IRREPS] = (lane // (LANES // 2)).astype(jnp.float32).astype(jnp.bfloat16)

    @pl.loop(0, most)
    def _(s):
        rows = pl.ds(pl.multiple_of(s * occupied, occupied), occupied)
        for label in range(IRREPS):
            for tile in range(tiles):
                acc[label, tile, rows, :] = jnp.zeros((occupied, LANES), jnp.float32)

    most = count[IRREPS]

    first_half = codes[IRREPS] == 0
    first_turned = pltpu.roll(codes[IRREPS], LANES // 2, 1) == 1

    def paired(first, second):
        turned = pltpu.roll(second, LANES // 2, second.ndim - 1)
        mask = first_half if first.ndim == 2 else jnp.broadcast_to(first_turned[None], first.shape)
        return jnp.where(mask, first, turned), jnp.where(mask, turned, first)

    def labels_of(block, m):
        c_label = vir_irrep[(place[0] + block // blocks_c * cs) // TILE]
        first = 2 * (block % blocks_c * per_block + m)
        return [jnp.bitwise_xor(c_label, vir_irrep[first + h]) for h in range(2)]

    def build(tp, block, m, base, slots):
        labels = labels_of(jnp.minimum(block, total - 1), m)
        lanes = slice(m * LANES, (m + 1) * LANES)
        z = jnp.where(first_half, codes[labels[0]], codes[labels[1]])
        masks = [z == x for x in range(IRREPS - 1)]
        held = block % 2
        for s in slots:
            ids = [table[(base + s) * IRREPS + x] for x in range(IRREPS)]
            merged = []
            for c in range(cs):
                out = t_buf[held, c, ids[IRREPS - 1], :, lanes]
                for x in range(IRREPS - 1):
                    out = jnp.where(masks[x], t_buf[held, c, ids[x], :, lanes], out)
                merged.append(out)
            for p in range(cs // 2):
                halves = paired(merged[2 * p], merged[2 * p + 1])
                for h in range(2):
                    tp[h, p, s * occupied:(s + 1) * occupied, :] = halves[h]

    def work(size, base, block, m):
        rows_all = size * occupied
        labels = labels_of(block, m)
        held = block % 2
        lanes = slice(m * LANES, (m + 1) * LANES)
        tp, after = tps[m], (m + 1) % per_block
        at = pl.ds(pl.multiple_of(base * occupied, occupied), rows_all)
        bands = virtual // band
        for n in range(bands):
            blocks = [v_buf[held, c, n * band:(n + 1) * band, :, lanes] for c in range(cs)]
            pairs = [paired(blocks[2 * p], blocks[2 * p + 1]) for p in range(cs // 2)]
            for h in range(2):
                weights = jnp.concatenate([pair[h].reshape(2 * LANES, LANES) for pair in pairs], axis=1)
                rows = jnp.concatenate([tp[h, p, :rows_all, :] for p in range(cs // 2)], axis=1)
                part = lax.dot_general(
                    rows, weights, (((1,), (1,)), ((), ())), preferred_element_type=jnp.float32
                )
                acc[labels[h], 2 * n, at, :] += part[:, :LANES]
                acc[labels[h], 2 * n + 1, at, :] += part[:, LANES:]
            build(tps[after], block + (after == 0), after, base, range(n * size // bands, (n + 1) * size // bands))

    def run(size, base):
        wait_all(0, 0)
        build(tps[0], 0, 0, base, range(size))

        @pl.loop(0, total)
        def _(block):
            @pl.when(block + 1 < total)
            def _():
                start_all(1, block + 1)

            wait_all(1, block)
            for m in range(per_block):
                if m == per_block - 1:
                    @pl.when(block + 2 < total)
                    def _():
                        start_all(0, block + 2)

                    @pl.when(block + 1 < total)
                    def _():
                        wait_all(0, block + 1)

                work(size, base, block, m)

    def begin():
        start_all(0, 0)
        start_all(1, 0)
        start_all(0, 1)

    low = 0
    for size in SIZES:
        @pl.when((most > low) & (most <= size))
        def _(size=size):
            run(size, 0)
        low = size

    @pl.when(most > low)
    def _():
        @pl.loop(0, (most + CHUNK - 1) // CHUNK)
        def _(r):
            @pl.when(r > 0)
            def _():
                begin()

            run(CHUNK, r * CHUNK)

    @pl.loop(0, occupied)
    def _(i):
        x = occ_irrep[i]
        rows = pl.ds(pl.multiple_of(slot_of[i] * occupied, occupied), occupied)
        to = pl.ds(pl.multiple_of(i * occupied, occupied), occupied)
        hit = [ycode_ref[...] == jnp.bitwise_xor(x, label) for label in range(IRREPS - 1)]
        for tile in range(tiles):
            out = acc[IRREPS - 1, tile, rows, :]
            for label in range(IRREPS - 1):
                out = jnp.where(hit[label], acc[label, tile, rows, :], out)
            xs[tile, to, :] = out

    @pl.loop(0, occupied * occupied // LANES)
    def _(r):
        rows = pl.ds(pl.multiple_of(r * LANES, LANES), LANES)
        for tile in range(tiles):
            zs[tile * LANES:(tile + 1) * LANES, :] = xs[tile, rows, :].T
        for tile in range(tiles):
            mixed = jnp.concatenate(
                [zs[pl.ds(tile * per_tile + b, virtual, stride=virtual), :] for b in range(per_tile)], axis=0
            )
            acc[0, tile, rows, :] = mixed.T

    near = occ_local // 2
    for part in range(2):
        @pl.loop(0, occupied // occ_local * near)
        def _(r, part=part):
            i = r // near * occ_local + part * near + r % near
            there = jnp.bitwise_xor(r // near, place[1])
            if part == 0 and occupied == 4 * occ_local:
                there = there % 2 * 2 + there // 2
            to = pl.ds(pl.multiple_of(r % near * occupied, occupied), occupied)
            rows = pl.ds(pl.multiple_of(i * occupied, occupied), occupied)
            for far in range(tiles):
                tile = jnp.bitwise_xor(place[2], far)
                value = xs[tile, rows, :] + acc[0, tile, pl.ds(i, occupied, stride=occupied), :]
                out_refs[2 * part + far % 2][there, far // 2, to, :] = value


def ladder(amplitudes, ladder_integrals, occ_irrep, vir_tile_irrep, first_c, occ_at, vir_at, occ_local):
    occupied, _, cd_local = amplitudes.shape
    virtual = ladder_integrals.shape[0]
    local_c = cd_local // NV
    cs = math.gcd(local_c, TILE, 4)
    assert cs % 2 == 0 and local_c * NV == cd_local and occupied == virtual and LANES % virtual == 0
    steps = local_c // cs
    assert steps * (NV // LANES) >= 4
    tiles = virtual * virtual // LANES
    place = jnp.stack([first_c, occ_at, vir_at] + [0 * occ_at] * 5)
    facts = jnp.concatenate([place, occ_irrep, vir_tile_irrep]).astype(jnp.int32)
    ycode = jnp.broadcast_to(occ_irrep[:, None], (occupied, LANES)).astype(jnp.int32)

    piece = jax.ShapeDtypeStruct(
        (occupied // occ_local, tiles // 2, occ_local // 2 * occupied, LANES), jnp.float32
    )
    slots = -(-occupied // CHUNK) * CHUNK
    return pl.pallas_call(
        functools.partial(ladder_kernel, cs=cs, occ_local=occ_local, steps=steps),
        out_shape=(piece,) * 4,
        grid_spec=pltpu.PrefetchScalarGridSpec(
            num_scalar_prefetch=1,
            grid=(),
            in_specs=[pl.BlockSpec(memory_space=pltpu.VMEM)] + [pl.BlockSpec(memory_space=pl.ANY)] * 2,
            out_specs=(pl.BlockSpec(memory_space=pltpu.VMEM),) * 4,
            scratch_shapes=[
                pltpu.VMEM((2, cs, occupied, occupied, STEPS * LANES), jnp.bfloat16),
                pltpu.VMEM((2, cs, virtual, virtual, STEPS * LANES), jnp.bfloat16),
                pltpu.VMEM((IRREPS, tiles, slots * occupied, LANES), jnp.float32),
                *[pltpu.VMEM((2, cs // 2, CHUNK * occupied, LANES), jnp.bfloat16)] * STEPS,
                pltpu.VMEM((tiles * LANES, LANES), jnp.float32),
                pltpu.VMEM((tiles, occupied * occupied, LANES), jnp.float32),
                pltpu.VMEM((IRREPS + 1, occupied, LANES), jnp.bfloat16),
                pltpu.SMEM((slots * IRREPS,), jnp.int32),
                pltpu.SMEM((occupied,), jnp.int32),
                pltpu.SMEM((8,), jnp.int32),
                pltpu.SemaphoreType.DMA((2, 2, cs)),
            ],
        ),
        compiler_params=pltpu.CompilerParams(vmem_limit_bytes=45 * 1024 * 1024),
    )(facts, ycode, amplitudes, ladder_integrals)


def swap(values, axis, bit):
    size = lax.axis_size(axis)
    return lax.ppermute(values, axis, [(n, n ^ bit) for n in range(size)])


def owned_sum(pieces):
    arrived = [swap(pieces[2 * part + 1], "vir", 1) for part in range(2)]
    order = [(1, 2), (2, 1)]
    near, first, second = [], [], []
    for part in range(2):
        kept, came = pieces[2 * part], arrived[part]
        low, far = lax.optimization_barrier((kept[:2] + came[:2], kept[2:] + came[2:]))
        near.append(low)
        first.append(swap(far, "occ", order[part][0]))
    for part in range(2):
        low, far = lax.optimization_barrier((near[part][0] + first[part][0], near[part][1] + first[part][1]))
        near[part] = low
        second.append(swap(far, "occ", order[part][1]))
    mine = jnp.stack([near[part] + second[part] for part in range(2)], axis=1)
    total = mine[0]
    for away in range(1, mine.shape[0]):
        total = total + swap(mine[away], "vir", 2 * away)
    return total


def local(amplitudes, ladder_integrals, driver, occ_energy, vir_energy, occ_irrep, vir_tile_irrep):
    occ_groups = lax.axis_size("occ")
    vir_groups = lax.axis_size("vir")
    occupied = amplitudes.shape[0]
    virtual = ladder_integrals.shape[0]
    occ_local = occupied // occ_groups
    vir_local = virtual // vir_groups
    rank = lax.axis_index(("occ", "vir"))
    occ_rank = lax.axis_index("occ")
    vir_rank = lax.axis_index("vir")
    first_c = rank * (amplitudes.shape[2] // NV)
    tiles = virtual * virtual // LANES
    direct = vir_groups == tiles == 8 and occ_groups == 4
    here = (occ_rank, vir_rank) if direct else (0 * occ_rank, 0 * vir_rank)
    pieces = ladder(amplitudes, ladder_integrals, occ_irrep, vir_tile_irrep, first_c, *here, occ_local)
    if direct:
        owned = owned_sum(pieces).reshape(occ_local, occupied, vir_local, virtual)
    else:
        halves = [jnp.stack([pieces[2 * p], pieces[2 * p + 1]], axis=2) for p in range(2)]
        if occ_groups == 4:
            halves[0] = halves[0][jnp.array([0, 2, 1, 3])]
        term = jnp.stack(halves, axis=3).transpose(1, 2, 0, 3, 4, 5).reshape(
            tiles, occ_groups, occ_local, occupied, vir_groups // tiles, vir_local, virtual
        )
        term = term.transpose(1, 0, 4, 2, 3, 5, 6).reshape(
            occ_groups * vir_groups, occ_local, occupied, vir_local, virtual
        )
        owned = lax.psum_scatter(term, ("occ", "vir"), scatter_dimension=0, tiled=True)[0]
    own_occ = lax.dynamic_slice_in_dim(occ_energy, occ_rank * occ_local, occ_local, 0)
    own_vir = lax.dynamic_slice_in_dim(vir_energy, vir_rank * vir_local, vir_local, 0)
    denom = (
        own_occ[:, None, None, None]
        + occ_energy[None, None, :, None]
        - own_vir[None, :, None, None]
        - vir_energy[None, None, None, :]
    )
    shaped = driver.reshape(occ_local, vir_local, occupied, virtual) + owned.transpose(0, 2, 1, 3)
    return (shaped / denom).reshape(occ_local, vir_local, occupied * virtual)


def solution(mesh):
    return jax.shard_map(
        local,
        mesh=mesh,
        in_specs=(
            P(None, None, ("occ", "vir")),
            P(None, None, ("occ", "vir")),
            P("occ", "vir", None),
            P(),
            P(),
            P(),
            P(),
        ),
        out_specs=P("occ", "vir", None),
        check_vma=False,
    )
```
